256 devices in a mesh: lat: 16 (over z, x_hi), lon: 16 (over y, x_lo, core).
Axes of the slice: x: 4 (x_hi: 2, x_lo: 2; x = x_hi * 2 + x_lo), y: 4, z: 8, core: 2. Of those that a mesh axis runs over, the one named last changes fastest.
Arguments:
- fields: bfloat16 [4, 96, 192, 384], P(None, 'lat', 'lon'), may hold values from -6 to 6
- cotangent: bfloat16 [4, 96, 192, 384], P(None, 'lat', 'lon'), may hold values from -6 to 6
- window_mask: int32 [2, 16, 16], P(None, 'lat', 'lon'), may hold values 0 or 1
- mask_token: bfloat16 [384], replicated, may hold values from -4 to 4
- norm_gain: bfloat16 [384], replicated, may hold values from 0.5 to 1.5
- qkv_weight: bfloat16 [1152, 384], replicated, may hold values from -0.3125 to 0.3125
- out_weight: bfloat16 [384, 384], replicated, may hold values from -0.3125 to 0.3125
- bias_table: float32 [16, 12, 759], P('lat'), may hold values from -300 to 300
- bias_index: int32 [144, 144], replicated, may hold values from 0 to 758
Outputs:
- output: bfloat16 [4, 96, 192, 384], P(None, 'lat', 'lon')
- input_grad: bfloat16 [4, 96, 192, 384], P(None, 'lat', 'lon')
- weight_grads: float32 [1536, 384], P(('lat', 'lon'))
- table_grad: float32 [16, 12, 759], P('lat')
- vector_grads: float32 [2, 384], replicated
The draws below stay inside these ranges and needn't reach their ends.
All inputs are finite; a program needn't handle non-finite values. No bound on the sum of `window_mask` on one device may be relied on, other than what follows from the above.
Results may differ from the reference program's by a relative error of at most 0.02.
Values may be sent and summed in bfloat16 or wider, within the bound.
No kernel may reach another device: no remote copies, remote signals or barrier semaphores. Data moves between devices by JAX's collectives and lax.ppermute only.
A program may use at most 64 MiB of HBM per device.

```python
import jax
import jax.numpy as jnp
from jax import lax

D = 384
HEADS = 12
HEAD_DIM = 32
WIN_Z = 2
WIN_LAT = 6
WIN_LON = 12
WIN_TOK = 144
NBIAS = 759
LEVELS = 4
NLAT = 96
NLON = 192
LAT_WIN = 16


def draw_bias_table(key, part):
    key = jax.random.fold_in(key, 7)
    shape = (LAT_WIN, HEADS, NBIAS)
    return jax.random.normal(key, shape, jnp.float32)


def touch_ends(result, key, low, largest):
    longest = result.shape.index(max(result.shape))
    spots = []
    for shift in (0, 1):
        where = [jax.random.randint(jax.random.fold_in(key, axis), (), 0, length) for axis, length in enumerate(result.shape)]
        where[longest] = (where[longest] + shift) % result.shape[longest]
        spots.append(tuple(where))
    return result.at[spots[0]].set(low).at[spots[1]].set(largest)


def level_of(rng, shape, cuts, low, largest):
    loudness = 1.0
    for dim, shards_of in cuts:
        heights = jax.random.uniform(jax.random.fold_in(jax.random.fold_in(rng, 6), dim), (shards_of,), jnp.float32, low / len(cuts), largest / len(cuts))
        loudness = loudness * jnp.repeat(jnp.exp(heights), shape[dim] // shards_of).reshape((-1,) + (1,) * (len(shape) - 1 - dim))
    return loudness


def normal_values(rng, shape, width, limit, cuts=(), held_as=jnp.bfloat16):
    values = jax.random.normal(rng, shape, jnp.float32) * width
    if len(cuts) > 0:
        values = level_of(rng, shape, cuts, -0.22, 0.18) * values
    return jnp.clip(values, min=-limit, max=limit).astype(held_as)


def setup_inputs(seed: int = 0) -> dict:
    seeds = jax.random.split(jax.random.key(seed), 10)
    fields = normal_values(seeds[0], (LEVELS, NLAT, NLON, D), 1.0, 6.0, ((1, 16), (2, 16)))
    cotangent = normal_values(seeds[1], (LEVELS, NLAT, NLON, D), 1.0, 6.0, ((1, 16), (2, 16)))
    window_mask = touch_ends((jax.random.randint(seeds[2], (LEVELS // WIN_Z, NLAT // WIN_LAT, NLON // WIN_LON), 0, 2) < 1).astype(jnp.int32), jax.random.fold_in(seeds[2], 1), 0, 1)
    mask_token = normal_values(seeds[3], (D,), 1.0, 4.0)
    norm_gain = jnp.clip(1.0 + 0.1 * jax.random.normal(seeds[4], (D,), jnp.float32), 0.5, 1.5).astype(jnp.bfloat16)
    qkv_weight = normal_values(seeds[5], (3 * D, D), D ** -0.5, 0.3125)
    out_weight = normal_values(seeds[6], (D, D), D ** -0.5, 0.3125)
    bias_table = draw_bias_table(jax.random.fold_in(seeds[9], 71), 0)
    bias_index = touch_ends(jax.random.randint(seeds[8], (WIN_TOK, WIN_TOK), 0, NBIAS), jax.random.fold_in(seeds[8], 1), 0, NBIAS - 1).astype(jnp.int32)
    return dict(fields=fields, cotangent=cotangent, window_mask=window_mask, mask_token=mask_token, norm_gain=norm_gain, qkv_weight=qkv_weight, out_weight=out_weight, bias_table=bias_table, bias_index=bias_index)


EPS = 1e-05
BLOCKED = -10000.0

def expand_mask(window_mask):
    spread = jnp.repeat(window_mask, WIN_Z, axis=0)
    spread = jnp.repeat(spread, WIN_LAT, axis=1)
    return jnp.repeat(spread, WIN_LON, axis=2)

def region_of(coords, extent, window):
    return (coords >= extent - window).astype(jnp.int32) + (coords >= extent - window // 2).astype(jnp.int32)

def to_windows(value):
    level_count, row_count, col_count, chan_count = value.shape
    value = value.reshape(level_count // WIN_Z, WIN_Z, row_count // WIN_LAT, WIN_LAT, col_count // WIN_LON, WIN_LON, chan_count)
    value = value.transpose(2, 0, 4, 1, 3, 5, 6)
    return value.reshape(row_count // WIN_LAT, level_count // WIN_Z * (col_count // WIN_LON), WIN_TOK, chan_count)

def from_windows(value, level_count, col_count):
    row_groups = value.shape[0]
    chan_count = value.shape[3]
    value = value.reshape(row_groups, level_count // WIN_Z, col_count // WIN_LON, WIN_Z, WIN_LAT, WIN_LON, chan_count)
    value = value.transpose(1, 3, 0, 4, 2, 5, 6)
    return value.reshape(level_count, row_groups * WIN_LAT, col_count, chan_count)

def window_block(tokens_win, cot_win, bias, regions, qkv_weight, out_weight):
    wide = jnp.float32
    low = jnp.bfloat16
    groups = tokens_win.shape[0]
    members = tokens_win.shape[1]
    scale = HEAD_DIM ** (-0.5)
    projected = jnp.einsum('rmtd,fd->rmtf', tokens_win.astype(wide), qkv_weight.astype(wide)).astype(low)
    projected = projected.reshape(groups, members, WIN_TOK, 3, HEADS, HEAD_DIM)
    queries = projected[:, :, :, 0]
    key_rows = projected[:, :, :, 1]
    values = projected[:, :, :, 2]
    scores = jnp.einsum('rmthe,rmshe->rmhts', queries.astype(wide), key_rows.astype(wide)) * scale + bias[:, None]
    apart = regions[:, :, :, None] != regions[:, :, None, :]
    scores = jnp.where(apart[:, :, None], BLOCKED, scores)
    row_max = lax.optimization_barrier(jnp.max(scores, axis=-1, keepdims=True))
    exponent = jnp.exp(scores - row_max)
    attn_prob = (exponent / lax.optimization_barrier(jnp.sum(exponent, axis=-1, keepdims=True))).astype(low)
    mixed_heads = jnp.einsum('rmhts,rmshe->rmthe', attn_prob.astype(wide), values.astype(wide)).astype(low)
    mixed_heads = mixed_heads.reshape(groups, members, WIN_TOK, HEADS * HEAD_DIM)
    branch = jnp.einsum('rmtd,fd->rmtf', mixed_heads.astype(wide), out_weight.astype(wide)).astype(low)
    out_grad = jnp.einsum('rmtf,rmtd->fd', cot_win.astype(wide), mixed_heads.astype(wide))
    grad_mixed = jnp.einsum('rmtf,fd->rmtd', cot_win.astype(wide), out_weight.astype(wide)).astype(low)
    grad_mixed = grad_mixed.reshape(groups, members, WIN_TOK, HEADS, HEAD_DIM)
    grad_attn = jnp.einsum('rmthe,rmshe->rmhts', grad_mixed.astype(wide), values.astype(wide))
    grad_values = jnp.einsum('rmhts,rmthe->rmshe', attn_prob.astype(wide), grad_mixed.astype(wide)).astype(low)
    prob_float = attn_prob.astype(wide)
    grad_scores = prob_float * (grad_attn - lax.optimization_barrier(jnp.sum(prob_float * grad_attn, axis=-1, keepdims=True)))
    bias_grad = lax.optimization_barrier(jnp.sum(grad_scores, axis=1))
    scores_low = grad_scores.astype(low)
    grad_queries = (jnp.einsum('rmhts,rmshe->rmthe', scores_low.astype(wide), key_rows.astype(wide)) * scale).astype(low)
    grad_keys = (jnp.einsum('rmhts,rmthe->rmshe', scores_low.astype(wide), queries.astype(wide)) * scale).astype(low)
    grad_qkv = jnp.stack((grad_queries, grad_keys, grad_values), axis=3).reshape(groups, members, WIN_TOK, 3 * HEADS * HEAD_DIM)
    qkv_grad = jnp.einsum('rmtf,rmtd->fd', grad_qkv.astype(wide), tokens_win.astype(wide))
    grad_tokens = jnp.einsum('rmtf,fd->rmtd', grad_qkv.astype(wide), qkv_weight.astype(wide)).astype(low)
    return (branch, grad_tokens, qkv_grad, out_grad, bias_grad)

def reference(fields, cotangent, window_mask, mask_token, norm_gain, qkv_weight, out_weight, bias_table, bias_index):
    wide = jnp.float32
    masked = expand_mask(window_mask) == 1
    filled = jnp.where(masked[..., None], mask_token, fields)
    filled_wide = filled.astype(wide)
    center = filled_wide - lax.optimization_barrier(jnp.mean(filled_wide, axis=-1, keepdims=True))
    inv_std = lax.rsqrt(lax.optimization_barrier(jnp.mean(center * center, axis=-1, keepdims=True)) + EPS)
    standard = center * inv_std
    normed = (standard * norm_gain.astype(wide)).astype(jnp.bfloat16)
    offsets = (-(WIN_Z // 2), -(WIN_LAT // 2), -(WIN_LON // 2))
    backs = (WIN_Z // 2, WIN_LAT // 2, WIN_LON // 2)
    shifted = jnp.roll(normed, offsets, axis=(0, 1, 2))
    shifted_cot = jnp.roll(cotangent, offsets, axis=(0, 1, 2))
    level_ids = region_of(jnp.arange(LEVELS, dtype=jnp.int32), LEVELS, WIN_Z)
    lat_ids = region_of(jnp.arange(NLAT, dtype=jnp.int32), NLAT, WIN_LAT)
    regions = level_ids[:, None] * 3 + lat_ids[None, :]
    region_field = jnp.broadcast_to(regions[:, :, None, None], (LEVELS, NLAT, NLON, 1))
    region_win = to_windows(region_field)[..., 0]
    bias = jnp.take(bias_table, bias_index.reshape(-1), axis=2).reshape(LAT_WIN, HEADS, WIN_TOK, WIN_TOK)

    def one_row(items):
        tokens_row, cot_row, bias_row, region_row = items
        outs = window_block(tokens_row[None], cot_row[None], bias_row[None], region_row[None], qkv_weight, out_weight)
        return (outs[0][0], outs[1][0], outs[2], outs[3], outs[4][0])
    branch_win, grad_win, qkv_parts, out_parts, bias_grad = lax.map(one_row, (to_windows(shifted), to_windows(shifted_cot), bias, region_win))
    qkv_grad = lax.optimization_barrier(jnp.sum(qkv_parts, axis=0))
    out_grad = lax.optimization_barrier(jnp.sum(out_parts, axis=0))
    branch = jnp.roll(from_windows(branch_win, LEVELS, NLON), backs, axis=(0, 1, 2))
    grad_normed = jnp.roll(from_windows(grad_win, LEVELS, NLON), backs, axis=(0, 1, 2))
    output = (filled_wide + branch.astype(wide)).astype(jnp.bfloat16)
    scaled = grad_normed.astype(wide) * norm_gain.astype(wide)
    grad_filled = cotangent.astype(wide) + inv_std * (scaled - lax.optimization_barrier(jnp.mean(scaled, axis=-1, keepdims=True)) - standard * lax.optimization_barrier(jnp.mean(scaled * standard, axis=-1, keepdims=True)))
    input_grad = jnp.where(masked[..., None], 0.0, grad_filled).astype(jnp.bfloat16)
    gain_grad = lax.optimization_barrier(jnp.sum(grad_normed.astype(wide) * standard, axis=(0, 1, 2)))
    token_grad = lax.optimization_barrier(jnp.sum(jnp.where(masked[..., None], grad_filled, 0.0), axis=(0, 1, 2)))
    vector_grads = jnp.stack((gain_grad, token_grad))
    flat_grad = bias_grad.reshape(LAT_WIN * HEADS, WIN_TOK * WIN_TOK).T
    table_grad = jax.ops.segment_sum(flat_grad, bias_index.reshape(-1), num_segments=NBIAS).T.reshape(LAT_WIN, HEADS, NBIAS)
    weight_grads = jnp.concatenate((qkv_grad, out_grad), axis=0)
    return (output, input_grad, weight_grads, table_grad, vector_grads)
```

```python
import functools

import jax
import jax.numpy as jnp
from jax import lax
from jax.experimental import pallas as pl
from jax.experimental.pallas import tpu as pltpu
from jax.sharding import PartitionSpec as P

HEADS = 12
HEAD_DIM = 32
WIN_TOK = 144
NBIAS = 759
D = 384
TOK = 288
EPS = 1e-05
BLOCKED = -10000.0
MARK = 256.0
LANES = 128
QSLOTS = 8
CHUNK = 128

wide = jnp.float32
low = jnp.bfloat16

NN = (((1,), (0,)), ((), ()))
NT = (((1,), (1,)), ((), ()))
TN = (((0,), (0,)), ((), ()))


def mm(a, b, dims):
    return lax.dot_general(a, b, dims, preferred_element_type=wide)


def passed_along(value, axis, steps):
    count = lax.axis_size(axis)
    pairs = [(source, (source + steps) % count) for source in range(count)]
    return lax.ppermute(value, axis, pairs)


def bias_kernel(table_ref, ids_ref, bias_ref):
    def rows(step, _):
        at = pl.ds(pl.multiple_of(step * 8, 8), 8)
        for half in range(2):
            cols = slice(half * LANES, (half + 1) * LANES)
            ids = ids_ref[at, cols]
            place = ids & (LANES - 1)
            piece = ids >> 7
            picks = [piece == p for p in range(6)]
            for head in range(HEADS):
                got = jnp.zeros((8, LANES), wide)
                for p in range(6):
                    source = jnp.broadcast_to(
                        table_ref[head : head + 1, p * LANES : (p + 1) * LANES], (8, LANES)
                    )
                    found = jnp.take_along_axis(source, place, axis=1)
                    got = jnp.where(picks[p], found, got)
                bias_ref[head, at, cols] = got
        return 0

    lax.fori_loop(0, WIN_TOK // 8, rows, 0)


def main_kernel(
    scal_ref,
    fields_ref,
    cot_ref,
    lat_ref,
    lon_ref,
    token_ref,
    gain_ref,
    wqkv_ref,
    wout_ref,
    bias_ref,
    ids_ref,
    out_own_ref,
    out_lat_ref,
    send_ref,
    x_ref,
    c_ref,
    std_ref,
    qkv_ref,
    gm_ref,
    qt_ref,
    gmt_ref,
    mixed_ref,
    gq_ref,
    gkt_ref,
    gvt_ref,
    bg_ref,
    fin_ref,
):
    for which, own, dest in ((0, fields_ref, x_ref), (1, cot_ref, c_ref)):
        for zs in range(4):
            z = (zs + 1) % 4
            for a in range(6):
                base = zs * 72 + a * 12
                if a < 3:
                    piece = own[z, 3 + a].astype(wide)[6:12]
                    if which == 0:
                        piece = jnp.where(scal_ref[z // 2] == 1, MARK, piece)
                else:
                    piece = lat_ref[which, z, a - 3].astype(wide)[6:12]
                dest[base : base + 6, :] = piece
                dest[base + 6 : base + 12, :] = lon_ref[which, z, a].astype(wide)
    raw = x_ref[...]
    masked = raw > 0.5 * MARK
    filled = jnp.where(masked, token_ref[...], raw)
    x_ref[...] = filled
    gain = gain_ref[...]
    center = filled - jnp.mean(filled, axis=-1, keepdims=True)
    inv_std = lax.rsqrt(jnp.mean(center * center, axis=-1, keepdims=True) + EPS)
    standard = center * inv_std
    std_ref[...] = standard
    normed = (standard * gain).astype(low)
    cot = c_ref[...].astype(low)

    qkv_ref[...] = mm(normed, wqkv_ref[...], NT).astype(low)
    gm_ref[...] = mm(cot, wout_ref[...], NN).astype(low)
    qt_ref[...] = mm(wqkv_ref[0:D, :], normed, NT).astype(low)
    gmt_ref[...] = mm(wout_ref[...], cot, (((0,), (1,)), ((), ()))).astype(low)

    last = scal_ref[2] == 1
    ti = lax.broadcasted_iota(jnp.int32, (WIN_TOK, WIN_TOK), 0)
    tj = lax.broadcasted_iota(jnp.int32, (WIN_TOK, WIN_TOK), 1)
    zi = (ti >= 72).astype(jnp.int32)
    zj = (tj >= 72).astype(jnp.int32)
    ai = (ti - 72 * zi >= 36).astype(jnp.int32)
    aj = (tj - 72 * zj >= 36).astype(jnp.int32)
    lat_apart = jnp.where(last, (ai != aj).astype(wide), 0.0)
    lev_apart = (zi != zj).astype(wide)
    apart = (lat_apart > 0.0, lat_apart + lev_apart > 0.0)
    lane = lax.broadcasted_iota(jnp.int32, (1, LANES), 1) // HEAD_DIM
    scale = HEAD_DIM ** (-0.5)
    for group in range(3):
        cols = slice(group * LANES, (group + 1) * LANES)
        for sub in range(4):
            head = group * 4 + sub
            mask = (lane == sub).astype(low)
            feats = slice(head * HEAD_DIM, (head + 1) * HEAD_DIM)
            bias = bias_ref[head, :, 0:WIN_TOK]
            total = None
            for w in range(2):
                rows = slice(w * WIN_TOK, (w + 1) * WIN_TOK)
                q = qkv_ref[rows, group * LANES : (group + 1) * LANES] * mask
                k = qkv_ref[rows, D + group * LANES : D + (group + 1) * LANES] * mask
                v = qkv_ref[rows, 2 * D + group * LANES : 2 * D + (group + 1) * LANES] * mask
                g = gm_ref[rows, cols]
                scores = mm(q, k, NT) * scale + bias
                scores = jnp.where(apart[w], BLOCKED, scores)
                top = jnp.max(scores, axis=-1, keepdims=True)
                expo = jnp.exp(scores - top)
                prob = (expo * (1.0 / jnp.sum(expo, axis=-1, keepdims=True))).astype(low)
                mixed = mm(prob, v, NN)
                grad_attn = mm(g, v, NT)
                gvt_ref[feats, rows] = mm(gmt_ref[feats, rows], prob, NN).astype(low)
                pf = prob.astype(wide)
                grad = pf * (grad_attn - jnp.sum(pf * grad_attn, axis=-1, keepdims=True))
                total = grad if total is None else total + grad
                glow = grad.astype(low)
                gq = mm(glow, k, NN)
                gkt_ref[feats, rows] = (mm(qt_ref[feats, rows], glow, NN) * scale).astype(low)
                if sub == 0:
                    mixed_ref[rows, cols] = mixed
                    gq_ref[rows, cols] = gq
                else:
                    mixed_ref[rows, cols] += mixed
                    gq_ref[rows, cols] += gq
            bg_ref[head] = total

    mixed = mixed_ref[...].astype(low)
    branch = mm(mixed, wout_ref[...], NT).astype(low).astype(wide)
    fin_ref[0] = x_ref[...] + branch

    gq = (gq_ref[...] * scale).astype(low)
    gk = gkt_ref[...].T
    gv = gvt_ref[...].T
    grad_normed = (
        mm(gq, wqkv_ref[0:D, :], NN)
        + mm(gk, wqkv_ref[D : 2 * D, :], NN)
        + mm(gv, wqkv_ref[2 * D : 3 * D, :], NN)
    )
    grad_normed = grad_normed.astype(low).astype(wide)
    standard = std_ref[...]
    scaled = grad_normed * gain
    inner = (
        scaled
        - jnp.mean(scaled, axis=-1, keepdims=True)
        - standard * jnp.mean(scaled * standard, axis=-1, keepdims=True)
    )
    grad_filled = c_ref[...] + inv_std * inner
    fin_ref[1] = jnp.where(masked, 0.0, grad_filled)
    gain_grad = jnp.sum(grad_normed * standard, axis=0, keepdims=True)
    token_grad = jnp.sum(jnp.where(masked, grad_filled, 0.0), axis=0, keepdims=True)

    for which in range(2):
        for zs in range(4):
            z = (zs + 1) % 4
            for a in range(6):
                base = zs * 72 + a * 12
                piece = fin_ref[which, base : base + 12, :].astype(low)
                if a < 3:
                    out_own_ref[which, z, a] = piece
                else:
                    out_lat_ref[which, z, a - 3] = piece

    new = lax.broadcasted_iota(jnp.int32, (D, D), 0)
    old = lax.broadcasted_iota(jnp.int32, (D, D), 1)
    o_new = new // 24
    rest = new - o_new * 24
    a_new = rest // 6
    order = (old == a_new * 96 + o_new * 6 + (rest - a_new * 6)).astype(low)
    parts = []
    for value in (gq, gk, gv, cot):
        turned = mm(order, value, NT).astype(low)
        other = mixed if value is cot else normed
        parts.append(mm(turned, other, NN))
    for o in range(16):
        rows = slice(o * 24, (o + 1) * 24)
        chunk = jnp.concatenate([part[rows] for part in parts], axis=0)
        send_ref[o, 0:96, :] = chunk.astype(low)

    slot = lax.broadcasted_iota(jnp.int32, (QSLOTS, WIN_TOK), 0)
    spot = lax.broadcasted_iota(jnp.int32, (LANES, WIN_TOK), 0)

    def one_row(i, acc):
        ids = ids_ref[pl.ds(i, 1), 0:WIN_TOK]
        near = (ids & (LANES - 1)) == spot
        right = near.astype(wide).astype(low)
        here = (ids >> 7) == slot
        left = jnp.concatenate(
            [
                jnp.where(here, bg_ref[head, pl.ds(i, 1), :], 0.0)
                for head in range(HEADS)
            ],
            axis=0,
        ).astype(low)
        return acc + mm(left, right, NT)

    acc = lax.fori_loop(0, WIN_TOK, one_row, jnp.zeros((HEADS * QSLOTS, LANES), wide))
    row = lax.broadcasted_iota(jnp.int32, (HEADS * QSLOTS, 1), 0)
    for n, vec in enumerate((gain_grad, token_grad)):
        for p in range(3):
            at = row == QSLOTS * p + 6 + n
            acc = jnp.where(at, vec[:, p * LANES : (p + 1) * LANES], acc)
    extra = jnp.concatenate([acc[0:32], acc[32:64], acc[64:96]], axis=1).astype(low)
    for o in range(16):
        send_ref[o, 96:128, :] = extra


def local(
    fields,
    cotangent,
    window_mask,
    mask_token,
    norm_gain,
    qkv_weight,
    out_weight,
    bias_table,
    bias_index,
):
    own_mask = window_mask[:, 0, 0]
    last = (lax.axis_index("lat") == lax.axis_size("lat") - 1).astype(jnp.int32)
    scalars = jnp.concatenate([own_mask, last[None], last[None]])
    level_mask = jnp.repeat(own_mask, 2)[:, None, None, None] == 1
    marked = jnp.where(level_mask, jnp.bfloat16(MARK), fields)

    strip = jnp.stack((marked[:, :3], cotangent[:, :3]))
    lat_in = passed_along(strip, "lat", -1)

    table = jnp.pad(bias_table[0], ((0, 0), (0, 9)))
    ids = jnp.pad(bias_index, ((0, 0), (0, 256 - WIN_TOK)))
    vmem = pl.BlockSpec(memory_space=pltpu.VMEM)
    bias = pl.pallas_call(
        bias_kernel,
        out_shape=jax.ShapeDtypeStruct((HEADS, WIN_TOK, 256), wide),
        in_specs=[vmem, vmem],
        out_specs=vmem,
        compiler_params=pltpu.CompilerParams(vmem_limit_bytes=32 * 2**20),
        cost_estimate=pl.CostEstimate(flops=10**7, bytes_accessed=6 * 10**6, transcendentals=0),
    )(table, ids)

    own = jnp.stack((marked[:, 3:, :6], cotangent[:, 3:, :6]))
    lon_in = passed_along(jnp.concatenate((own, lat_in[:, :, :, :6]), axis=2), "lon", -1)

    out_own, out_lat, send = pl.pallas_call(
        main_kernel,
        out_shape=(
            jax.ShapeDtypeStruct((2, 4, 3, 12, D), low),
            jax.ShapeDtypeStruct((2, 4, 3, 12, D), low),
            jax.ShapeDtypeStruct((16, CHUNK, D), low),
        ),
        in_specs=[pl.BlockSpec(memory_space=pltpu.SMEM)] + [vmem] * 10,
        out_specs=(vmem, vmem, vmem),
        scratch_shapes=[
            pltpu.VMEM((TOK, D), wide),
            pltpu.VMEM((TOK, D), wide),
            pltpu.VMEM((TOK, D), wide),
            pltpu.VMEM((TOK, 3 * D), low),
            pltpu.VMEM((TOK, D), low),
            pltpu.VMEM((D, TOK), low),
            pltpu.VMEM((D, TOK), low),
            pltpu.VMEM((TOK, D), wide),
            pltpu.VMEM((TOK, D), wide),
            pltpu.VMEM((D, TOK), low),
            pltpu.VMEM((D, TOK), low),
            pltpu.VMEM((HEADS, WIN_TOK, WIN_TOK), wide),
            pltpu.VMEM((2, TOK, D), wide),
        ],
        compiler_params=pltpu.CompilerParams(vmem_limit_bytes=48 * 2**20),
        cost_estimate=pl.CostEstimate(
            flops=2 * 10**9, bytes_accessed=10**7, transcendentals=5 * 10**5
        ),
    )(
        scalars,
        fields,
        cotangent,
        lat_in,
        lon_in,
        mask_token.astype(wide)[None],
        norm_gain.astype(wide)[None],
        qkv_weight,
        out_weight,
        bias,
        ids,
    )

    lat_out = passed_along(out_lat, "lat", 1)
    full = jnp.concatenate((lat_out, out_own), axis=2)
    lon_out = passed_along(full[:, :, :, 6:], "lon", 1)

    got = lax.all_to_all(send, "lon", 0, 0, tiled=True)
    summed = jnp.sum(got.astype(wide), axis=0)
    extra = summed[96:].reshape(32, 3, LANES).transpose(1, 0, 2).reshape(HEADS, QSLOTS, LANES)
    table_grad = extra[:, :6].reshape(1, HEADS, 6 * LANES)[:, :, :NBIAS]
    vectors = extra[:3, 6:].transpose(1, 0, 2).reshape(2, D)
    second = jnp.concatenate(
        (summed[:96].reshape(16, 6, D), jnp.broadcast_to(vectors[None], (16, 2, D))), axis=1
    ).astype(low)
    final = jnp.sum(lax.all_to_all(second, "lat", 0, 0, tiled=True).astype(wide), axis=0)

    output = jnp.concatenate((lon_out[0], full[0, :, :, :6]), axis=2)
    input_grad = jnp.concatenate((lon_out[1], full[1, :, :, :6]), axis=2)
    return (output, input_grad, final[:6], table_grad, final[6:])


def solution(mesh):
    placed = (
        P(None, "lat", "lon", None),
        P(None, "lat", "lon", None),
        P(None, "lat", "lon"),
        P(),
        P(),
        P(),
        P(),
        P("lat", None, None),
        P(),
    )
    return jax.shard_map(
        local,
        mesh=mesh,
        in_specs=placed,
        out_specs=(
            P(None, "lat", "lon", None),
            P(None, "lat", "lon", None),
            P(("lat", "lon"), None),
            P("lat", None, None),
            P(),
        ),
        check_vma=False,
    )
```

```python
import functools

import jax
import jax.numpy as jnp
from jax import lax
from jax.experimental import pallas as pl
from jax.experimental.pallas import tpu as pltpu
from jax.sharding import PartitionSpec as P

HEADS = 12
HEAD_DIM = 32
WIN_TOK = 144
NBIAS = 759
D = 384
TOK = 288
EPS = 1e-05
BLOCKED = -10000.0
MARK = 256.0
LANES = 128
QSLOTS = 8
CHUNK = 128

wide = jnp.float32
low = jnp.bfloat16

NN = (((1,), (0,)), ((), ()))
NT = (((1,), (1,)), ((), ()))
TN = (((0,), (0,)), ((), ()))


def mm(a, b, dims):
    return lax.dot_general(a, b, dims, preferred_element_type=wide)


def passed_along(value, axis, steps):
    count = lax.axis_size(axis)
    pairs = [(source, (source + steps) % count) for source in range(count)]
    return lax.ppermute(value, axis, pairs)


def bias_kernel(table_ref, ids_ref, bias_ref):
    def rows(step, _):
        at = pl.ds(pl.multiple_of(step * 8, 8), 8)
        for half in range(2):
            cols = slice(half * LANES, (half + 1) * LANES)
            ids = ids_ref[at, cols]
            place = ids & (LANES - 1)
            piece = ids >> 7
            picks = [piece == p for p in range(6)]
            for head in range(HEADS):
                got = jnp.zeros((8, LANES), wide)
                for p in range(6):
                    source = jnp.broadcast_to(
                        table_ref[head : head + 1, p * LANES : (p + 1) * LANES], (8, LANES)
                    )
                    found = jnp.take_along_axis(source, place, axis=1)
                    got = jnp.where(picks[p], found, got)
                bias_ref[head, at, cols] = got
        return 0

    lax.fori_loop(0, WIN_TOK // 8, rows, 0)


def main_kernel(
    scal_ref,
    fields_ref,
    cot_ref,
    lat_ref,
    lon_ref,
    token_ref,
    gain_ref,
    wqkv_ref,
    wout_ref,
    bias_ref,
    ids_ref,
    rest_ref,
    out_own_ref,
    out_lat_ref,
    keep_ref,
    give_ref,
    x_ref,
    c_ref,
    std_ref,
    qkv_ref,
    gm_ref,
    qt_ref,
    gmt_ref,
    mixed_ref,
    gq_ref,
    gkt_ref,
    gvt_ref,
    bg_ref,
    bt_ref,
    rem_ref,
    mix_ref,
):
    level = lax.broadcasted_iota(jnp.int32, (4, 1), 0)
    own_masked = jnp.where(level < 2, scal_ref[0], scal_ref[1]) == 1
    for which, own, dest in ((0, fields_ref, x_ref), (1, cot_ref, c_ref)):
        for a in range(6):
            for o in range(12):
                if o >= 6:
                    piece = lon_ref[which, a, o - 6]
                elif a >= 3:
                    piece = lat_ref[which, a - 3, 6 + o]
                else:
                    piece = own[3 + a, 6 + o]
                piece = piece.astype(wide)
                if which == 0 and o < 6 and a < 3:
                    piece = jnp.where(own_masked, MARK, piece)
                base = (a * 12 + o) * 4
                for c in range(3):
                    mix_ref[c, base : base + 4, :] = piece[:, c * LANES : (c + 1) * LANES]
        for zs in range(4):
            for c in range(3):
                dest[zs * 72 : (zs + 1) * 72, c * LANES : (c + 1) * LANES] = mix_ref[
                    c, pl.ds((zs + 1) % 4, 72, stride=4), :
                ]
    raw = x_ref[...]
    masked = raw > 0.5 * MARK
    filled = jnp.where(masked, token_ref[...], raw)
    x_ref[...] = filled
    gain = gain_ref[...]
    center = filled - jnp.mean(filled, axis=-1, keepdims=True)
    inv_std = lax.rsqrt(jnp.mean(center * center, axis=-1, keepdims=True) + EPS)
    standard = center * inv_std
    std_ref[...] = standard
    normed = (standard * gain).astype(low)
    cot = c_ref[...].astype(low)

    qkv_ref[...] = mm(normed, wqkv_ref[...], NT).astype(low)
    gm_ref[...] = mm(cot, wout_ref[...], NN).astype(low)
    for w in range(2):
        rows = slice(w * WIN_TOK, (w + 1) * WIN_TOK)
        qt_ref[w] = mm(wqkv_ref[0:D, :], normed[rows], NT).astype(low)
        gmt_ref[w] = mm(wout_ref[...], cot[rows], (((0,), (1,)), ((), ()))).astype(low)

    last = scal_ref[2] == 1
    ti = lax.broadcasted_iota(jnp.int32, (WIN_TOK, WIN_TOK), 0)
    tj = lax.broadcasted_iota(jnp.int32, (WIN_TOK, WIN_TOK), 1)
    zi = (ti >= 72).astype(jnp.int32)
    zj = (tj >= 72).astype(jnp.int32)
    ai = (ti - 72 * zi >= 36).astype(jnp.int32)
    aj = (tj - 72 * zj >= 36).astype(jnp.int32)
    lat_apart = jnp.where(last, (ai != aj).astype(wide), 0.0)
    lev_apart = (zi != zj).astype(wide)
    apart = (lat_apart > 0.0, lat_apart + lev_apart > 0.0)
    lane = lax.broadcasted_iota(jnp.int32, (1, LANES), 1) // HEAD_DIM
    scale = HEAD_DIM ** (-0.5)
    for group in range(3):
        cols = slice(group * LANES, (group + 1) * LANES)
        mixed_sum = [None, None]
        gq_sum = [None, None]
        for sub in range(4):
            head = group * 4 + sub
            mask = (lane == sub).astype(low)
            feats = slice(head * HEAD_DIM, (head + 1) * HEAD_DIM)
            bias = bias_ref[head, :, 0:WIN_TOK]
            total = None
            for w in range(2):
                rows = slice(w * WIN_TOK, (w + 1) * WIN_TOK)
                q = qkv_ref[rows, group * LANES : (group + 1) * LANES] * mask
                k = qkv_ref[rows, D + group * LANES : D + (group + 1) * LANES] * mask
                v = qkv_ref[rows, 2 * D + group * LANES : 2 * D + (group + 1) * LANES] * mask
                g = gm_ref[rows, cols]
                scores = mm(q, k, NT) * scale + bias
                scores = jnp.where(apart[w], BLOCKED, scores)
                top = jnp.max(scores, axis=-1, keepdims=True)
                expo = jnp.exp(scores - top)
                prob = (expo * (1.0 / jnp.sum(expo, axis=-1, keepdims=True))).astype(low)
                mixed = mm(prob, v, NN)
                grad_attn = mm(g, v, NT)
                gvt_ref[w, feats, :] = mm(gmt_ref[w, feats, :], prob, NN).astype(low)
                delta = jnp.sum(g.astype(wide) * mixed, axis=-1, keepdims=True)
                grad = prob.astype(wide) * (grad_attn - delta)
                total = grad if total is None else total + grad
                glow = grad.astype(low)
                gq = mm(glow, k, NN)
                gkt_ref[w, feats, :] = (mm(qt_ref[w, feats, :], glow, NN) * scale).astype(low)
                mixed_sum[w] = mixed if sub == 0 else mixed_sum[w] + mixed
                gq_sum[w] = gq if sub == 0 else gq_sum[w] + gq
            bg_ref[head] = total[:, 0:LANES]
            bt_ref[head, :, 0:16] = total[:, LANES:WIN_TOK]
        for w in range(2):
            rows = slice(w * WIN_TOK, (w + 1) * WIN_TOK)
            mixed_ref[rows, cols] = mixed_sum[w].astype(low)
            gq_ref[rows, cols] = (gq_sum[w] * scale).astype(low)

    def put_back(which, value):
        for zs in range(4):
            for c in range(3):
                mix_ref[c, pl.ds((zs + 1) % 4, 72, stride=4), :] = value[
                    zs * 72 : (zs + 1) * 72, c * LANES : (c + 1) * LANES
                ]
        for a in range(6):
            for o in range(12):
                base = (a * 12 + o) * 4
                piece = jnp.concatenate([mix_ref[c, base : base + 4, :] for c in range(3)], axis=1)
                if a < 3:
                    out_own_ref[which, a, o] = piece.astype(low)
                else:
                    out_lat_ref[which, a - 3, o] = piece.astype(low)

    mixed = mixed_ref[...]
    branch = mm(mixed, wout_ref[...], NT).astype(low).astype(wide)
    put_back(0, x_ref[...] + branch)

    gq = gq_ref[...]
    gk = jnp.concatenate([gkt_ref[w].T for w in range(2)], axis=0)
    gv = jnp.concatenate([gvt_ref[w].T for w in range(2)], axis=0)
    grad_normed = (
        mm(gq, wqkv_ref[0:D, :], NN)
        + mm(gk, wqkv_ref[D : 2 * D, :], NN)
        + mm(gv, wqkv_ref[2 * D : 3 * D, :], NN)
    )
    grad_normed = grad_normed.astype(low).astype(wide)
    standard = std_ref[...]
    scaled = grad_normed * gain
    inner = (
        scaled
        - jnp.mean(scaled, axis=-1, keepdims=True)
        - standard * jnp.mean(scaled * standard, axis=-1, keepdims=True)
    )
    grad_filled = c_ref[...] + inv_std * inner
    put_back(1, jnp.where(masked, 0.0, grad_filled))
    gain_grad = jnp.sum(grad_normed * standard, axis=0, keepdims=True)
    token_grad = jnp.sum(jnp.where(masked, grad_filled, 0.0), axis=0, keepdims=True)

    new = lax.broadcasted_iota(jnp.int32, (D, D), 0)
    old = lax.broadcasted_iota(jnp.int32, (D, D), 1)
    n_new = new // 24
    rest = new - n_new * 24
    half = n_new // 8
    core = scal_ref[3]
    o_new = 2 * (n_new - 8 * half) + (core + half - 2 * core * half)
    a_new = rest // 6
    order = (old == a_new * 96 + o_new * 6 + (rest - a_new * 6)).astype(low)
    parts = []
    for value in (gq, gk, gv, cot):
        turned = mm(order, value, NT).astype(low)
        other = mixed if value is cot else normed
        parts.append(mm(turned, other, NN))
    for o in range(16):
        rows = slice(o * 24, (o + 1) * 24)
        chunk = jnp.concatenate([part[rows] for part in parts], axis=0)
        dest = keep_ref if o < 8 else give_ref
        dest[o % 8, 0:96, :] = chunk.astype(low)

    slot = lax.broadcasted_iota(jnp.int32, (QSLOTS, LANES), 0)
    spot = lax.broadcasted_iota(jnp.int32, (LANES, LANES), 0)
    for head in range(HEADS):
        rem_ref[head] = jnp.concatenate(
            [bt_ref[head, pl.ds(k, 18, stride=8), :][:, 0:16] for k in range(8)], axis=1
        )

    def one_step(step, acc):
        lefts = []
        rights = []
        for s in range(9):
            if s < 8:
                ids = ids_ref[pl.ds(step * 8 + s, 1), :]
                vals = [bg_ref[head, pl.ds(step * 8 + s, 1), :] for head in range(HEADS)]
            else:
                ids = rest_ref[pl.ds(step, 1), :]
                vals = [rem_ref[head, pl.ds(step, 1), :] for head in range(HEADS)]
            rights.append(((ids & (LANES - 1)) == spot).astype(wide).astype(low))
            here = (ids >> 7) == slot
            lefts.append(
                jnp.concatenate([jnp.where(here, val, 0.0) for val in vals], axis=0).astype(low)
            )
        left = jnp.concatenate(lefts, axis=1)
        right = jnp.concatenate(rights, axis=1)
        return acc + mm(left, right, NT)

    acc = lax.fori_loop(0, 18, one_step, jnp.zeros((HEADS * QSLOTS, LANES), wide))
    row = lax.broadcasted_iota(jnp.int32, (HEADS * QSLOTS, 1), 0)
    for n, vec in enumerate((gain_grad, token_grad)):
        for p in range(3):
            at = row == QSLOTS * p + 6 + n
            acc = jnp.where(at, vec[:, p * LANES : (p + 1) * LANES], acc)
    extra = jnp.concatenate([acc[0:32], acc[32:64], acc[64:96]], axis=1).astype(low)
    for n in range(8):
        keep_ref[n, 96:128, :] = extra
        give_ref[n, 96:128, :] = extra


def local(
    fields,
    cotangent,
    window_mask,
    mask_token,
    norm_gain,
    qkv_weight,
    out_weight,
    bias_table,
    bias_index,
):
    own_mask = window_mask[:, 0, 0]
    last = lax.axis_index("lat") == lax.axis_size("lat") - 1
    core = lax.axis_index("lon") % 2
    scalars = jnp.concatenate([own_mask, jnp.stack([last.astype(jnp.int32), core])])
    fields = fields.transpose(1, 2, 0, 3)
    cotangent = cotangent.transpose(1, 2, 0, 3)
    hidden = jnp.repeat(own_mask, 2)[:, None] == 1
    strip = jnp.stack((jnp.where(hidden, jnp.bfloat16(MARK), fields[:3]), cotangent[:3]))
    lat_in = passed_along(strip, "lat", -1)

    table = jnp.pad(bias_table[0], ((0, 0), (0, 9)))
    ids = jnp.pad(bias_index, ((0, 0), (0, 256 - WIN_TOK)))
    vmem = pl.BlockSpec(memory_space=pltpu.VMEM)
    bias = pl.pallas_call(
        bias_kernel,
        out_shape=jax.ShapeDtypeStruct((HEADS, WIN_TOK, 256), wide),
        in_specs=[vmem, vmem],
        out_specs=vmem,
        compiler_params=pltpu.CompilerParams(vmem_limit_bytes=8 * 2**20),
        cost_estimate=pl.CostEstimate(flops=10**7, bytes_accessed=6 * 10**6, transcendentals=0),
    )(table, ids)

    lat_in, bias = lax.optimization_barrier((lat_in, bias))
    own = jnp.stack((jnp.where(hidden, jnp.bfloat16(MARK), fields[3:, :6]), cotangent[3:, :6]))
    lon_in = passed_along(jnp.concatenate((own, lat_in[:, :, :6]), axis=1), "lon", -1)

    out_own, out_lat, keep, give = pl.pallas_call(
        main_kernel,
        out_shape=(
            jax.ShapeDtypeStruct((2, 3, 12, 4, D), low),
            jax.ShapeDtypeStruct((2, 3, 12, 4, D), low),
            jax.ShapeDtypeStruct((8, CHUNK, D), low),
            jax.ShapeDtypeStruct((8, CHUNK, D), low),
        ),
        in_specs=[pl.BlockSpec(memory_space=pltpu.SMEM)] + [vmem] * 11,
        out_specs=(vmem, vmem, vmem, vmem),
        scratch_shapes=[
            pltpu.VMEM((TOK, D), wide),
            pltpu.VMEM((TOK, D), wide),
            pltpu.VMEM((TOK, D), wide),
            pltpu.VMEM((TOK, 3 * D), low),
            pltpu.VMEM((TOK, D), low),
            pltpu.VMEM((2, D, WIN_TOK), low),
            pltpu.VMEM((2, D, WIN_TOK), low),
            pltpu.VMEM((TOK, D), low),
            pltpu.VMEM((TOK, D), low),
            pltpu.VMEM((2, D, WIN_TOK), low),
            pltpu.VMEM((2, D, WIN_TOK), low),
            pltpu.VMEM((HEADS, WIN_TOK, LANES), wide),
            pltpu.VMEM((HEADS, WIN_TOK, LANES), wide),
            pltpu.VMEM((HEADS, 18, LANES), wide),
            pltpu.VMEM((3, TOK, LANES), wide),
        ],
        compiler_params=pltpu.CompilerParams(vmem_limit_bytes=24 * 2**20),
        cost_estimate=pl.CostEstimate(
            flops=2 * 10**9, bytes_accessed=10**7, transcendentals=5 * 10**5
        ),
    )(
        scalars,
        fields,
        cotangent,
        lat_in,
        lon_in,
        mask_token.astype(wide)[None],
        norm_gain.astype(wide)[None],
        qkv_weight,
        out_weight,
        bias,
        bias_index[:, :LANES],
        bias_index[:, LANES:].reshape(18, 8 * 16),
    )

    size = lax.axis_size("lon")
    taken = lax.ppermute(give, "lon", [(i, i ^ 1) for i in range(size)])
    lat_out = passed_along(out_lat, "lat", 1)
    pair = (keep.astype(wide) + taken.astype(wide)).astype(low)
    groups = [list(range(c, size, 2)) for c in range(2)]
    got = lax.all_to_all(pair, "lon", 0, 0, axis_index_groups=groups, tiled=True)
    summed = jnp.sum(got.astype(wide), axis=0)
    extra = summed[96:].reshape(32, 3, LANES).transpose(1, 0, 2).reshape(HEADS, QSLOTS, LANES)
    table_grad = extra[:, :6].reshape(1, HEADS, 6 * LANES)[:, :, :NBIAS]
    vectors = extra[:3, 6:].transpose(1, 0, 2).reshape(2, D)
    second = jnp.concatenate(
        (summed[:96].reshape(16, 6, D), jnp.broadcast_to(vectors[None], (16, 2, D))), axis=1
    ).astype(low)
    full = jnp.concatenate((lat_out, out_own), axis=1)
    full, second = lax.optimization_barrier((full, second))
    lon_out = passed_along(full[:, :, 6:], "lon", 1)
    final = jnp.sum(lax.all_to_all(second, "lat", 0, 0, tiled=True).astype(wide), axis=0)
    done = jnp.concatenate((lon_out, full[:, :, :6]), axis=2).transpose(0, 3, 1, 2, 4)
    output, input_grad = done[0], done[1]
    return (output, input_grad, final[:6], table_grad, final[6:])


def solution(mesh):
    placed = (
        P(None, "lat", "lon", None),
        P(None, "lat", "lon", None),
        P(None, "lat", "lon"),
        P(),
        P(),
        P(),
        P(),
        P("lat", None, None),
        P(),
    )
    return jax.shard_map(
        local,
        mesh=mesh,
        in_specs=placed,
        out_specs=(
            P(None, "lat", "lon", None),
            P(None, "lat", "lon", None),
            P(("lat", "lon"), None),
            P("lat", None, None),
            P(),
        ),
        check_vma=False,
    )
```

```python
import functools

import jax
import jax.numpy as jnp
from jax import lax
from jax.experimental import pallas as pl
from jax.experimental.pallas import tpu as pltpu
from jax.sharding import PartitionSpec as P

HEADS = 12
HEAD_DIM = 32
WIN_TOK = 144
NBIAS = 759
D = 384
TOK = 288
EPS = 1e-05
BLOCKED = -10000.0
MARK = 256.0
LANES = 128
LOG2E = 1.4426950408889634
QSLOTS = 8
CHUNK = 56

wide = jnp.float32
low = jnp.bfloat16

NN = (((1,), (0,)), ((), ()))
NT = (((1,), (1,)), ((), ()))
TN = (((0,), (0,)), ((), ()))


def mm(a, b, dims):
    return lax.dot_general(a, b, dims, preferred_element_type=wide)


def passed_along(value, axis, steps):
    count = lax.axis_size(axis)
    pairs = [(source, (source + steps) % count) for source in range(count)]
    return lax.ppermute(value, axis, pairs)


def pre_kernel(scal_ref, table_ref, ids_ref, bias_ref, order_ref, tail_ref, far_ref):
    new = lax.broadcasted_iota(jnp.int32, (D, D), 0)
    old = lax.broadcasted_iota(jnp.int32, (D, D), 1)
    tens = new // 6
    r = new - 6 * tens
    zl = tens & 1
    xh = (tens >> 1) & 1
    j = (tens >> 2) & 7
    other = tens >> 5
    core = scal_ref[3]
    c = core + other - 2 * core * other
    order_ref[...] = (old == ((2 * zl + xh) * 16 + 2 * j + c) * 6 + r).astype(wide).astype(low)

    tail_ref[...] = jnp.zeros((WIN_TOK, LANES), jnp.int32)
    tail_ref[:, 0:16] = ids_ref[:, LANES:WIN_TOK]
    for head in range(HEADS):
        for p in range(6):
            stop = min((p + 1) * LANES, NBIAS)
            far_ref[head * 6 + p : head * 6 + p + 1, 0 : stop - p * LANES] = (
                table_ref[head, :, p * LANES : stop] * LOG2E
            )

    def rows(step, _):
        at = pl.ds(pl.multiple_of(step * 8, 8), 8)
        for half in range(2):
            ids = ids_ref[at, 0:LANES] if half == 0 else tail_ref[at, :]
            place = ids & (LANES - 1)
            piece = ids >> 7
            picks = [piece == p for p in range(6)]
            for head in range(HEADS):
                got = None
                for p in range(6):
                    source = jnp.broadcast_to(
                        far_ref[head * 6 + p : head * 6 + p + 1, :], (8, LANES)
                    )
                    found = jnp.take_along_axis(source, place, axis=1)
                    got = found if got is None else jnp.where(picks[p], found, got)
                bias_ref[head, at, half * LANES : (half + 1) * LANES] = got
        return 0

    lax.fori_loop(0, WIN_TOK // 8, rows, 0)


def main_kernel(
    scal_ref,
    fields_ref,
    cot_ref,
    lat_ref,
    lon_ref,
    token_ref,
    gain_ref,
    wqkv_ref,
    wout_ref,
    bias_in_ref,
    order_ref,
    out_own_ref,
    out_lat_ref,
    keep_ref,
    give_ref,
    bg_ref,
    bt_ref,
    x_ref,
    c_ref,
    std_ref,
    qkv_ref,
    gm_ref,
    qt_ref,
    gmt_ref,
    mixed_ref,
    gq_ref,
    gkt_ref,
    gvt_ref,
    bias_ref,
    bias_sem,
    mix_ref,
):
    bias_copy = pltpu.make_async_copy(bias_in_ref, bias_ref, bias_sem)
    bias_copy.start()
    level = lax.broadcasted_iota(jnp.int32, (4, 1), 0)
    own_masked = jnp.where(level < 2, scal_ref[0], scal_ref[1]) == 1
    for which, own, dest in ((0, fields_ref, x_ref), (1, cot_ref, c_ref)):
        for a in range(6):
            for o in range(12):
                if o >= 6:
                    piece = lon_ref[which, a, o - 6]
                elif a >= 3:
                    piece = lat_ref[which, a - 3, 6 + o]
                else:
                    piece = own[3 + a, 6 + o]
                piece = piece.astype(wide)
                if which == 0 and o < 6 and a < 3:
                    piece = jnp.where(own_masked, MARK, piece)
                base = (a * 12 + o) * 4
                for c in range(3):
                    mix_ref[c, base : base + 4, :] = piece[:, c * LANES : (c + 1) * LANES]
        for zs in range(4):
            for c in range(3):
                dest[zs * 72 : (zs + 1) * 72, c * LANES : (c + 1) * LANES] = mix_ref[
                    c, pl.ds((zs + 1) % 4, 72, stride=4), :
                ]
    raw = x_ref[...]
    masked = raw > 0.5 * MARK
    filled = jnp.where(masked, token_ref[...], raw)
    x_ref[...] = filled
    gain = gain_ref[...]
    center = filled - jnp.mean(filled, axis=-1, keepdims=True)
    inv_std = lax.rsqrt(jnp.mean(center * center, axis=-1, keepdims=True) + EPS)
    standard = center * inv_std
    std_ref[...] = standard
    normed = (standard * gain).astype(low)
    cot = c_ref[...].astype(low)

    qkv_ref[...] = mm(normed, wqkv_ref[...], NT).astype(low)
    gm_ref[...] = mm(cot, wout_ref[...], NN).astype(low)
    for w in range(2):
        rows = slice(w * WIN_TOK, (w + 1) * WIN_TOK)
        qt_ref[w] = mm(wqkv_ref[0:D, :], normed[rows], NT).astype(low)
        gmt_ref[w] = mm(wout_ref[...], cot[rows], (((0,), (1,)), ((), ()))).astype(low)

    last = scal_ref[2] == 1
    ti = lax.broadcasted_iota(jnp.int32, (WIN_TOK, WIN_TOK), 0)
    tj = lax.broadcasted_iota(jnp.int32, (WIN_TOK, WIN_TOK), 1)
    zi = (ti >= 72).astype(jnp.int32)
    zj = (tj >= 72).astype(jnp.int32)
    ai = (ti - 72 * zi >= 36).astype(jnp.int32)
    aj = (tj - 72 * zj >= 36).astype(jnp.int32)
    lat_apart = jnp.where(last, (ai != aj).astype(wide), 0.0)
    lev_apart = (zi != zj).astype(wide)
    apart = (lat_apart > 0.0, lat_apart + lev_apart > 0.0)
    lane = lax.broadcasted_iota(jnp.int32, (1, LANES), 1) // HEAD_DIM
    scale = HEAD_DIM ** (-0.5)
    masks = [(lane == sub).astype(low) for sub in range(4)]
    bias_copy.wait()
    for group in range(3):
        cols = slice(group * LANES, (group + 1) * LANES)
        kcols = slice(D + group * LANES, D + (group + 1) * LANES)
        vcols = slice(2 * D + group * LANES, 2 * D + (group + 1) * LANES)
        totals = [None] * 4
        for w in range(2):
            rows = slice(w * WIN_TOK, (w + 1) * WIN_TOK)
            q = qkv_ref[rows, cols]
            k = qkv_ref[rows, kcols]
            v = qkv_ref[rows, vcols]
            g = gm_ref[rows, cols]
            raw_scores = mm(jnp.concatenate([q * mask for mask in masks], axis=0), k, NT)
            raw_grads = mm(jnp.concatenate([g * mask for mask in masks], axis=0), v, NT)
            g_wide = g.astype(wide)
            mixed_sum = None
            gq_sum = None
            for sub in range(4):
                head = group * 4 + sub
                feats = slice(head * HEAD_DIM, (head + 1) * HEAD_DIM)
                part = slice(sub * WIN_TOK, (sub + 1) * WIN_TOK)
                scores = raw_scores[part] * (scale * LOG2E) + bias_ref[head, :, 0:WIN_TOK]
                scores = jnp.where(apart[w], BLOCKED * LOG2E, scores)
                top = jnp.max(scores, axis=-1, keepdims=True)
                expo = jnp.exp2(scores - top)
                prob = (expo * (1.0 / jnp.sum(expo, axis=-1, keepdims=True))).astype(low)
                mixed = mm(prob, v * masks[sub], NN)
                gvt_ref[w, feats, :] = mm(gmt_ref[w, feats, :], prob, NN).astype(low)
                delta = jnp.sum(g_wide * mixed, axis=-1, keepdims=True)
                grad = prob.astype(wide) * (raw_grads[part] - delta)
                glow = grad.astype(low)
                gq = mm(glow, k * masks[sub], NN)
                gkt_ref[w, feats, :] = (mm(qt_ref[w, feats, :], glow, NN) * scale).astype(low)
                mixed_sum = mixed if sub == 0 else mixed_sum + mixed
                gq_sum = gq if sub == 0 else gq_sum + gq
                if w == 0:
                    totals[sub] = grad
                else:
                    total = totals[sub] + grad
                    bg_ref[head] = total[:, 0:LANES]
                    bt_ref[head, :, 0:16] = total[:, LANES:WIN_TOK]
            mixed_ref[rows, cols] = mixed_sum.astype(low)
            gq_ref[rows, cols] = (gq_sum * scale).astype(low)

    def put_back(which, value):
        for zs in range(4):
            for c in range(3):
                mix_ref[c, pl.ds((zs + 1) % 4, 72, stride=4), :] = value[
                    zs * 72 : (zs + 1) * 72, c * LANES : (c + 1) * LANES
                ]
        for a in range(6):
            for o in range(12):
                base = (a * 12 + o) * 4
                piece = jnp.concatenate([mix_ref[c, base : base + 4, :] for c in range(3)], axis=1)
                if a < 3:
                    out_own_ref[which, a, o] = piece.astype(low)
                else:
                    out_lat_ref[which, a - 3, o] = piece.astype(low)

    mixed = mixed_ref[...]
    branch = mm(mixed, wout_ref[...], NT).astype(low).astype(wide)
    put_back(0, x_ref[...] + branch)

    gq = gq_ref[...]
    gk = jnp.concatenate([gkt_ref[w].T for w in range(2)], axis=0)
    gv = jnp.concatenate([gvt_ref[w].T for w in range(2)], axis=0)
    grad_normed = (
        mm(gq, wqkv_ref[0:D, :], NN)
        + mm(gk, wqkv_ref[D : 2 * D, :], NN)
        + mm(gv, wqkv_ref[2 * D : 3 * D, :], NN)
    )
    grad_normed = grad_normed.astype(low).astype(wide)
    standard = std_ref[...]
    scaled = grad_normed * gain
    inner = (
        scaled
        - jnp.mean(scaled, axis=-1, keepdims=True)
        - standard * jnp.mean(scaled * standard, axis=-1, keepdims=True)
    )
    grad_filled = c_ref[...] + inv_std * inner
    put_back(1, jnp.where(masked, 0.0, grad_filled))
    gain_grad = jnp.sum(grad_normed * standard, axis=0, keepdims=True)
    token_grad = jnp.sum(jnp.where(masked, grad_filled, 0.0), axis=0, keepdims=True)

    order = order_ref[...]
    parts = []
    for value in (gq, gk, gv, cot):
        turned = mm(order, value, NT).astype(low)
        other = mixed if value is cot else normed
        parts.append(mm(turned, other, NN))
    vectors = jnp.concatenate([gain_grad, token_grad, jnp.zeros((6, D), wide)], axis=0)
    for n in range(32):
        rows = slice(n * 12, (n + 1) * 12)
        chunk = jnp.concatenate([part[rows] for part in parts] + [vectors], axis=0)
        dest = keep_ref if n < 16 else give_ref
        dest[n % 16] = chunk.astype(low)


def table_kernel(bg_ref, bt_ref, ids_ref, sums_ref, rem_ref, near_ref, tail_ref, rest_ref):
    slot = lax.broadcasted_iota(jnp.int32, (QSLOTS, LANES), 0)
    spot = lax.broadcasted_iota(jnp.int32, (LANES, LANES), 0)
    near_ref[...] = ids_ref[:, 0:LANES]
    tail_ref[:, 0:16] = ids_ref[:, LANES:WIN_TOK]
    rest_ref[...] = jnp.concatenate(
        [tail_ref[pl.ds(k, 18, stride=8), :][:, 0:16] for k in range(8)], axis=1
    )
    for head in range(HEADS):
        rem_ref[head] = jnp.concatenate(
            [bt_ref[head, pl.ds(k, 18, stride=8), :][:, 0:16] for k in range(8)], axis=1
        )

    def one_step(step, acc):
        lefts = []
        rights = []
        for s in range(9):
            if s < 8:
                ids = near_ref[pl.ds(step * 8 + s, 1), :]
                vals = [bg_ref[head, pl.ds(step * 8 + s, 1), :] for head in range(HEADS)]
            else:
                ids = rest_ref[pl.ds(step, 1), :]
                vals = [rem_ref[head, pl.ds(step, 1), :] for head in range(HEADS)]
            rights.append(((ids & (LANES - 1)) == spot).astype(wide).astype(low))
            here = (ids >> 7) == slot
            lefts.append(
                jnp.concatenate([jnp.where(here, val, 0.0) for val in vals], axis=0).astype(low)
            )
        left = jnp.concatenate(lefts, axis=1)
        right = jnp.concatenate(rights, axis=1)
        return acc + mm(left, right, NT)

    start = jnp.zeros((HEADS * QSLOTS, LANES), wide)
    sums_ref[...] = lax.fori_loop(0, 18, one_step, start, unroll=6)


def pack_kernel(keep_ref, taken_ref, table_ref, send_ref):
    total = keep_ref[0].astype(wide) + taken_ref[0].astype(wide)
    table = table_ref[...]
    row = lax.broadcasted_iota(jnp.int32, (HEADS * QSLOTS, 1), 0)
    for n in range(2):
        for p in range(3):
            piece = total[48 + n : 49 + n, p * LANES : (p + 1) * LANES]
            table = jnp.where(row == QSLOTS * p + 6 + n, piece, table)
    extra = jnp.concatenate([table[0:32], table[32:64], table[64:96]], axis=1).astype(low)
    for m in range(16):
        total = keep_ref[m].astype(wide) + taken_ref[m].astype(wide)
        send_ref[m, 0:48, :] = total[0:48].astype(low)
        send_ref[m, 48:80, :] = extra


def sum_kernel(scal_ref, got_ref, second_ref, table_ref):
    weights = got_ref[0, 0:48, :].astype(wide)
    for m in range(1, 16):
        weights = weights + got_ref[m, 0:48, :].astype(wide)
    sides = []
    for xh in range(2):
        side = got_ref[xh, 48:80, :].astype(wide)
        for j in range(1, 8):
            side = side + got_ref[2 * j + xh, 48:80, :].astype(wide)
        sides.append(side)
    table_ref[...] = jnp.where(scal_ref[4] == 0, sides[0], sides[1])
    both = sides[0] + sides[1]
    vectors = jnp.concatenate(
        [both[QSLOTS * p + 6 : QSLOTS * p + 8, 0:LANES] for p in range(3)], axis=1
    )
    for z in range(8):
        chunk = jnp.concatenate([weights[6 * z : 6 * z + 6], vectors], axis=0)
        second_ref[z] = chunk.astype(low)


def local(
    fields,
    cotangent,
    window_mask,
    mask_token,
    norm_gain,
    qkv_weight,
    out_weight,
    bias_table,
    bias_index,
):
    own_mask = window_mask[:, 0, 0]
    last = lax.axis_index("lat") == lax.axis_size("lat") - 1
    core = lax.axis_index("lon") % 2
    side = lax.axis_index("lat") % 2
    scalars = jnp.concatenate([own_mask, jnp.stack([last.astype(jnp.int32), core, side])])
    fields = fields.transpose(1, 2, 0, 3)
    cotangent = cotangent.transpose(1, 2, 0, 3)
    hidden = jnp.repeat(own_mask, 2)[:, None] == 1
    strip = jnp.stack((jnp.where(hidden, jnp.bfloat16(MARK), fields[:3]), cotangent[:3]))
    lat_in = passed_along(strip, "lat", -1)

    smem = pl.BlockSpec(memory_space=pltpu.SMEM)
    vmem = pl.BlockSpec(memory_space=pltpu.VMEM)
    bias, order = pl.pallas_call(
        pre_kernel,
        out_shape=(
            jax.ShapeDtypeStruct((HEADS, WIN_TOK, 256), wide),
            jax.ShapeDtypeStruct((D, D), low),
        ),
        in_specs=[smem, vmem, vmem],
        out_specs=(vmem,) * 2,
        scratch_shapes=[
            pltpu.VMEM((WIN_TOK, LANES), jnp.int32),
            pltpu.VMEM((HEADS * 6, LANES), wide),
        ],
        compiler_params=pltpu.CompilerParams(vmem_limit_bytes=8 * 2**20),
        cost_estimate=pl.CostEstimate(flops=10**7, bytes_accessed=6 * 10**6, transcendentals=0),
    )(scalars, bias_table.transpose(1, 0, 2), bias_index)
    lat_in, bias, order = lax.optimization_barrier((lat_in, bias, order))
    own = jnp.stack((jnp.where(hidden, jnp.bfloat16(MARK), fields[3:, :6]), cotangent[3:, :6]))
    lon_in = passed_along(jnp.concatenate((own, lat_in[:, :, :6]), axis=1), "lon", -1)

    out_own, out_lat, keep, give, bias_grad, bias_tail = pl.pallas_call(
        main_kernel,
        out_shape=(
            jax.ShapeDtypeStruct((2, 3, 12, 4, D), low),
            jax.ShapeDtypeStruct((2, 3, 12, 4, D), low),
            jax.ShapeDtypeStruct((16, CHUNK, D), low),
            jax.ShapeDtypeStruct((16, CHUNK, D), low),
            jax.ShapeDtypeStruct((HEADS, WIN_TOK, LANES), wide),
            jax.ShapeDtypeStruct((HEADS, WIN_TOK, LANES), wide),
        ),
        in_specs=[smem] + [vmem] * 8 + [pl.BlockSpec(memory_space=pl.ANY), vmem],
        out_specs=(vmem,) * 6,
        scratch_shapes=[
            pltpu.VMEM((TOK, D), wide),
            pltpu.VMEM((TOK, D), wide),
            pltpu.VMEM((TOK, D), wide),
            pltpu.VMEM((TOK, 3 * D), low),
            pltpu.VMEM((TOK, D), low),
            pltpu.VMEM((2, D, WIN_TOK), low),
            pltpu.VMEM((2, D, WIN_TOK), low),
            pltpu.VMEM((TOK, D), low),
            pltpu.VMEM((TOK, D), low),
            pltpu.VMEM((2, D, WIN_TOK), low),
            pltpu.VMEM((2, D, WIN_TOK), low),
            pltpu.VMEM((HEADS, WIN_TOK, 256), wide),
            pltpu.SemaphoreType.DMA(()),
            pltpu.VMEM((3, TOK, LANES), wide),
        ],
        compiler_params=pltpu.CompilerParams(vmem_limit_bytes=24 * 2**20),
        cost_estimate=pl.CostEstimate(
            flops=2 * 10**9, bytes_accessed=10**7, transcendentals=5 * 10**5
        ),
    )(
        scalars,
        fields,
        cotangent,
        lat_in,
        lon_in,
        mask_token.astype(wide)[None],
        norm_gain.astype(wide)[None],
        qkv_weight,
        out_weight,
        bias,
        order,
    )

    size = lax.axis_size("lon")
    bands = lax.axis_size("lat")

    def swapped(value, bit):
        return lax.ppermute(value, "lon", [(i, i ^ bit) for i in range(size)])

    taken = swapped(give, 1)
    lat_out = passed_along(out_lat, "lat", 1)
    table = pl.pallas_call(
        table_kernel,
        out_shape=jax.ShapeDtypeStruct((HEADS * QSLOTS, LANES), wide),
        in_specs=[vmem] * 3,
        out_specs=vmem,
        scratch_shapes=[
            pltpu.VMEM((HEADS, 18, LANES), wide),
            pltpu.VMEM((WIN_TOK, LANES), jnp.int32),
            pltpu.VMEM((WIN_TOK, LANES), jnp.int32),
            pltpu.VMEM((18, LANES), jnp.int32),
        ],
        compiler_params=pltpu.CompilerParams(vmem_limit_bytes=8 * 2**20),
        cost_estimate=pl.CostEstimate(flops=10**9, bytes_accessed=10**6, transcendentals=0),
    )(bias_grad, bias_tail, bias_index)
    pair = pl.pallas_call(
        pack_kernel,
        out_shape=jax.ShapeDtypeStruct((16, 80, D), low),
        in_specs=[vmem] * 3,
        out_specs=vmem,
        compiler_params=pltpu.CompilerParams(vmem_limit_bytes=8 * 2**20),
        cost_estimate=pl.CostEstimate(flops=10**6, bytes_accessed=10**6, transcendentals=0),
    )(keep, taken, table)
    groups = [
        [(2 * z + xh) * size + 2 * j + c for j in range(size // 2) for xh in range(2)]
        for z in range(bands // 2)
        for c in range(2)
    ]
    got = lax.all_to_all(pair, ("lat", "lon"), 0, 0, axis_index_groups=groups, tiled=True)
    second, table = pl.pallas_call(
        sum_kernel,
        out_shape=(
            jax.ShapeDtypeStruct((8, 8, D), low),
            jax.ShapeDtypeStruct((32, D), wide),
        ),
        in_specs=[smem, vmem],
        out_specs=(vmem, vmem),
        compiler_params=pltpu.CompilerParams(vmem_limit_bytes=8 * 2**20),
        cost_estimate=pl.CostEstimate(flops=10**6, bytes_accessed=10**6, transcendentals=0),
    )(scalars, got)

    full = jnp.concatenate((lat_out, out_own), axis=1)
    full, second = lax.optimization_barrier((full, second))
    groups = [[(2 * z + xh) for z in range(bands // 2)] for xh in range(2)]
    final = lax.all_to_all(second, "lat", 0, 0, axis_index_groups=groups, tiled=True)
    lon_out = passed_along(full[:, :, 6:], "lon", 1)
    table = table + swapped(table, 1)
    done = jnp.concatenate((lon_out, full[:, :, :6]), axis=2).transpose(0, 3, 1, 2, 4)
    output, input_grad = done[0], done[1]
    table = table.reshape(32, 3, LANES).transpose(1, 0, 2).reshape(HEADS, QSLOTS, LANES)
    table_grad = table[:, :6].reshape(1, HEADS, 6 * LANES)
    table_grad = table_grad[:, :, :NBIAS]
    final, output, input_grad, table_grad = lax.optimization_barrier(
        (final, output, input_grad, table_grad)
    )
    weight_grads = jnp.sum(final[:, :6].astype(wide), axis=0)
    vector_grads = jnp.sum(final[:, 6:].astype(wide), axis=0)
    return (output, input_grad, weight_grads, table_grad, vector_grads)


def solution(mesh):
    placed = (
        P(None, "lat", "lon", None),
        P(None, "lat", "lon", None),
        P(None, "lat", "lon"),
        P(),
        P(),
        P(),
        P(),
        P("lat", None, None),
        P(),
    )
    return jax.shard_map(
        local,
        mesh=mesh,
        in_specs=placed,
        out_specs=(
            P(None, "lat", "lon", None),
            P(None, "lat", "lon", None),
            P(("lat", "lon"), None),
            P("lat", None, None),
            P(),
        ),
        check_vma=False,
    )
```

```python
import functools

import jax
import jax.numpy as jnp
from jax import lax
from jax.experimental import pallas as pl
from jax.experimental.pallas import tpu as pltpu
from jax.sharding import PartitionSpec as P

HEADS = 12
HEAD_DIM = 32
WIN_TOK = 144
NBIAS = 759
D = 384
TOK = 288
EPS = 1e-05
BLOCKED = -10000.0
MARK = 256.0
LANES = 128
LOG2E = 1.4426950408889634
QSLOTS = 8
CHUNK = 104

wide = jnp.float32
low = jnp.bfloat16

NN = (((1,), (0,)), ((), ()))
NT = (((1,), (1,)), ((), ()))
TN = (((0,), (0,)), ((), ()))


def mm(a, b, dims):
    return lax.dot_general(a, b, dims, preferred_element_type=wide)


def passed_along(value, axis, steps):
    count = lax.axis_size(axis)
    pairs = [(source, (source + steps) % count) for source in range(count)]
    return lax.ppermute(value, axis, pairs)


def pre_kernel(
    place_ref, table_in, ids_in, bias_ref, order_ref, table_ref, ids_ref, tail_ref, far_ref, sems
):
    copies = [
        pltpu.make_async_copy(table_in, table_ref, sems.at[0]),
        pltpu.make_async_copy(ids_in, ids_ref, sems.at[1]),
    ]
    for copy in copies:
        copy.start()
    new = lax.broadcasted_iota(jnp.int32, (D, D), 0)
    old = lax.broadcasted_iota(jnp.int32, (D, D), 1)
    tens = new // 6
    r = new - 6 * tens
    a = tens & 3
    j = (tens >> 2) & 7
    other = tens >> 5
    core = place_ref[0]
    c = core + other - 2 * core * other
    order_ref[...] = (old == (a * 16 + 2 * j + c) * 6 + r).astype(wide).astype(low)

    for copy in copies:
        copy.wait()
    tail_ref[...] = jnp.zeros((WIN_TOK, LANES), jnp.int32)
    tail_ref[:, 0:16] = ids_ref[:, LANES:WIN_TOK]
    for head in range(HEADS):
        for p in range(6):
            stop = min((p + 1) * LANES, NBIAS)
            far_ref[head * 6 + p : head * 6 + p + 1, 0 : stop - p * LANES] = (
                table_ref[head, :, p * LANES : stop] * LOG2E
            )

    def rows(step, _):
        at = pl.ds(pl.multiple_of(step * 8, 8), 8)
        for half in range(2):
            ids = ids_ref[at, 0:LANES] if half == 0 else tail_ref[at, :]
            place = ids & (LANES - 1)
            piece = ids >> 7
            picks = [piece == p for p in range(6)]
            for head in range(HEADS):
                got = None
                for p in range(6):
                    source = jnp.broadcast_to(
                        far_ref[head * 6 + p : head * 6 + p + 1, :], (8, LANES)
                    )
                    found = jnp.take_along_axis(source, place, axis=1)
                    got = found if got is None else jnp.where(picks[p], found, got)
                bias_ref[head, at, half * LANES : (half + 1) * LANES] = got
        return 0

    lax.fori_loop(0, WIN_TOK // 8, rows, 0)


def main_kernel(
    place_ref,
    scal_ref,
    fields_ref,
    cot_ref,
    lat_ref,
    lon_ref,
    token_ref,
    gain_ref,
    wqkv_in_ref,
    wout_ref,
    bias_ref,
    order_ref,
    filled_ref,
    mixed_ref,
    igrad_ref,
    keep_ref,
    give_ref,
    bg_ref,
    bt_ref,
    x_ref,
    c_ref,
    std_ref,
    qkv_ref,
    gm_ref,
    qt_ref,
    gmt_ref,
    gq_ref,
    gkt_ref,
    gvt_ref,
    wqkv_ref,
    sem,
    mix_ref,
):
    wqkv_copy = pltpu.make_async_copy(wqkv_in_ref, wqkv_ref, sem)
    wqkv_copy.start()
    level = lax.broadcasted_iota(jnp.int32, (4, 1), 0)
    own_masked = jnp.where(level < 2, scal_ref[0], scal_ref[1]) == 1
    for which, own, dest in ((0, fields_ref, x_ref), (1, cot_ref, c_ref)):
        for a in range(6):
            for o in range(12):
                if o >= 6:
                    piece = lon_ref[which, a, o - 6]
                elif a >= 3:
                    piece = lat_ref[which, a - 3, 6 + o]
                else:
                    piece = own[3 + a, 6 + o]
                piece = piece.astype(wide)
                if which == 0 and o < 6 and a < 3:
                    piece = jnp.where(own_masked, MARK, piece)
                base = (a * 12 + o) * 4
                for c in range(3):
                    mix_ref[c, base : base + 4, :] = piece[:, c * LANES : (c + 1) * LANES]
        for zs in range(4):
            for c in range(3):
                dest[zs * 72 : (zs + 1) * 72, c * LANES : (c + 1) * LANES] = mix_ref[
                    c, pl.ds((zs + 1) % 4, 72, stride=4), :
                ]
    raw = x_ref[...]
    masked = raw > 0.5 * MARK
    filled = jnp.where(masked, token_ref[...], raw)
    filled_ref[...] = filled.astype(low)
    gain = gain_ref[...]
    center = filled - jnp.mean(filled, axis=-1, keepdims=True)
    inv_std = lax.rsqrt(jnp.mean(center * center, axis=-1, keepdims=True) + EPS)
    standard = center * inv_std
    std_ref[...] = standard
    normed = (standard * gain).astype(low)
    cot = c_ref[...].astype(low)

    wqkv_copy.wait()
    qkv_ref[...] = mm(normed, wqkv_ref[...], NT).astype(low)
    gm_ref[...] = mm(cot, wout_ref[...], NN).astype(low)
    for w in range(2):
        rows = slice(w * WIN_TOK, (w + 1) * WIN_TOK)
        qt_ref[w] = mm(wqkv_ref[0:D, :], normed[rows], NT).astype(low)
        gmt_ref[w] = mm(wout_ref[...], cot[rows], (((0,), (1,)), ((), ()))).astype(low)

    last = place_ref[1] == 1
    ti = lax.broadcasted_iota(jnp.int32, (WIN_TOK, WIN_TOK), 0)
    tj = lax.broadcasted_iota(jnp.int32, (WIN_TOK, WIN_TOK), 1)
    zi = (ti >= 72).astype(jnp.int32)
    zj = (tj >= 72).astype(jnp.int32)
    ai = (ti - 72 * zi >= 36).astype(jnp.int32)
    aj = (tj - 72 * zj >= 36).astype(jnp.int32)
    lat_apart = jnp.where(last, (ai != aj).astype(wide), 0.0)
    lev_apart = (zi != zj).astype(wide)
    apart = [
        jnp.concatenate([value] * 4, axis=0) > 0.0 for value in (lat_apart, lat_apart + lev_apart)
    ]
    lane = lax.broadcasted_iota(jnp.int32, (1, LANES), 1) // HEAD_DIM
    scale = HEAD_DIM ** (-0.5)
    masks = [(lane == sub).astype(low) for sub in range(4)]
    for group in range(3):
        cols = slice(group * LANES, (group + 1) * LANES)
        kcols = slice(D + group * LANES, D + (group + 1) * LANES)
        vcols = slice(2 * D + group * LANES, 2 * D + (group + 1) * LANES)
        totals = [None] * 4
        for w in range(2):
            rows = slice(w * WIN_TOK, (w + 1) * WIN_TOK)
            q = qkv_ref[rows, cols]
            k = qkv_ref[rows, kcols]
            v = qkv_ref[rows, vcols]
            g = gm_ref[rows, cols]
            q_four = jnp.concatenate([q * mask for mask in masks], axis=0)
            g_four = jnp.concatenate([g * mask for mask in masks], axis=0)
            biases = jnp.concatenate(
                [bias_ref[group * 4 + sub, :, 0:WIN_TOK] for sub in range(4)], axis=0
            )
            scores = mm(q_four, k, NT) * (scale * LOG2E) + biases
            scores = jnp.where(apart[w], BLOCKED * LOG2E, scores)
            top = jnp.max(scores, axis=-1, keepdims=True)
            expo = jnp.exp2(scores - top)
            prob = (expo * (1.0 / jnp.sum(expo, axis=-1, keepdims=True))).astype(low)
            mixed = mm(prob, v, NN)
            delta = jnp.sum(g_four.astype(wide) * mixed, axis=-1, keepdims=True)
            grad = prob.astype(wide) * (mm(g_four, v, NT) - delta)
            glow = grad.astype(low)
            gq = mm(glow, k, NN)
            mixed_sum = jnp.zeros((WIN_TOK, LANES), wide)
            gq_sum = jnp.zeros((WIN_TOK, LANES), wide)
            for sub in range(4):
                head = group * 4 + sub
                feats = slice(head * HEAD_DIM, (head + 1) * HEAD_DIM)
                part = slice(sub * WIN_TOK, (sub + 1) * WIN_TOK)
                mixed_sum = jnp.where(lane == sub, mixed[part], mixed_sum)
                gq_sum = jnp.where(lane == sub, gq[part], gq_sum)
                gvt_ref[w, feats, :] = mm(gmt_ref[w, feats, :], prob[part], NN).astype(low)
                gkt_ref[w, feats, :] = (mm(qt_ref[w, feats, :], glow[part], NN) * scale).astype(low)
                if w == 0:
                    totals[sub] = grad[part]
                else:
                    total = totals[sub] + grad[part]
                    bg_ref[head] = total[:, 0:LANES]
                    bt_ref[head, :, 0:16] = total[:, LANES:WIN_TOK]
            mixed_ref[rows, cols] = mixed_sum.astype(low)
            gq_ref[rows, cols] = (gq_sum * scale).astype(low)

    mixed = mixed_ref[...]
    gq = gq_ref[...]
    gk = jnp.concatenate([gkt_ref[w].T for w in range(2)], axis=0)
    gv = jnp.concatenate([gvt_ref[w].T for w in range(2)], axis=0)
    grad_normed = (
        mm(gq, wqkv_ref[0:D, :], NN)
        + mm(gk, wqkv_ref[D : 2 * D, :], NN)
        + mm(gv, wqkv_ref[2 * D : 3 * D, :], NN)
    )
    grad_normed = grad_normed.astype(low).astype(wide)
    standard = std_ref[...]
    scaled = grad_normed * gain
    inner = (
        scaled
        - jnp.mean(scaled, axis=-1, keepdims=True)
        - standard * jnp.mean(scaled * standard, axis=-1, keepdims=True)
    )
    grad_filled = c_ref[...] + inv_std * inner
    igrad_ref[...] = jnp.where(masked, 0.0, grad_filled).astype(low)
    gain_grad = jnp.sum(grad_normed * standard, axis=0, keepdims=True)
    token_grad = jnp.sum(jnp.where(masked, grad_filled, 0.0), axis=0, keepdims=True)

    order = order_ref[...]
    parts = []
    for value in (gq, gk, gv, cot):
        turned = mm(order, value, NT).astype(low)
        other = mixed if value is cot else normed
        parts.append(mm(turned, other, NN))
    vectors = jnp.concatenate([gain_grad, token_grad, jnp.zeros((6, D), wide)], axis=0)
    for n in range(16):
        rows = slice(n * 24, (n + 1) * 24)
        chunk = jnp.concatenate([part[rows] for part in parts] + [vectors], axis=0)
        dest = keep_ref if n < 8 else give_ref
        dest[n % 8] = chunk.astype(low)


def out_kernel(filled_ref, mixed_ref, igrad_ref, wout_ref, out_own_ref, out_lon_ref, mix_ref):
    def put_back(which, value):
        for zs in range(4):
            for c in range(3):
                mix_ref[c, pl.ds((zs + 1) % 4, 72, stride=4), :] = value[
                    zs * 72 : (zs + 1) * 72, c * LANES : (c + 1) * LANES
                ]
        for a in range(6):
            for o in range(12):
                base = (a * 12 + o) * 4
                piece = jnp.concatenate([mix_ref[c, base : base + 4, :] for c in range(3)], axis=1)
                if o < 6:
                    out_own_ref[which, a, o] = piece.astype(low)
                else:
                    out_lon_ref[which, a, o - 6] = piece.astype(low)

    branch = mm(mixed_ref[...], wout_ref[...], NT).astype(low).astype(wide)
    put_back(0, filled_ref[...].astype(wide) + branch)
    put_back(1, igrad_ref[...].astype(wide))


def table_kernel(bg_ref, bt_ref, ids_ref, sums_ref, rem_ref, near_ref, tail_ref, rest_ref):
    slot = lax.broadcasted_iota(jnp.int32, (QSLOTS, LANES), 0)
    spot = lax.broadcasted_iota(jnp.int32, (LANES, LANES), 0)
    near_ref[...] = ids_ref[:, 0:LANES]
    tail_ref[:, 0:16] = ids_ref[:, LANES:WIN_TOK]
    rest_ref[...] = jnp.concatenate(
        [tail_ref[pl.ds(k, 18, stride=8), :][:, 0:16] for k in range(8)], axis=1
    )
    for head in range(HEADS):
        rem_ref[head] = jnp.concatenate(
            [bt_ref[head, pl.ds(k, 18, stride=8), :][:, 0:16] for k in range(8)], axis=1
        )

    def one_step(step, acc):
        lefts = []
        rights = []
        for s in range(9):
            if s < 8:
                ids = near_ref[pl.ds(step * 8 + s, 1), :]
                vals = [bg_ref[head, pl.ds(step * 8 + s, 1), :] for head in range(HEADS)]
            else:
                ids = rest_ref[pl.ds(step, 1), :]
                vals = [rem_ref[head, pl.ds(step, 1), :] for head in range(HEADS)]
            rights.append(((ids & (LANES - 1)) == spot).astype(wide).astype(low))
            here = (ids >> 7) == slot
            lefts.append(
                jnp.concatenate([jnp.where(here, val, 0.0) for val in vals], axis=0).astype(low)
            )
        left = jnp.concatenate(lefts, axis=1)
        right = jnp.concatenate(rights, axis=1)
        return acc + mm(left, right, NT)

    start = jnp.zeros((HEADS * QSLOTS, LANES), wide)
    sums_ref[...] = lax.fori_loop(0, 18, one_step, start, unroll=6)


def pack_kernel(keep_ref, taken_ref, table_ref, send_ref):
    total = keep_ref[0].astype(wide) + taken_ref[0].astype(wide)
    table = table_ref[...]
    row = lax.broadcasted_iota(jnp.int32, (HEADS * QSLOTS, 1), 0)
    for n in range(2):
        for p in range(3):
            piece = total[96 + n : 97 + n, p * LANES : (p + 1) * LANES]
            table = jnp.where(row == QSLOTS * p + 6 + n, piece, table)
    extra = jnp.concatenate([table[0:32], table[32:64], table[64:96]], axis=1).astype(low)
    for m in range(8):
        total = keep_ref[m].astype(wide) + taken_ref[m].astype(wide)
        send_ref[m, 0:96, :] = total[0:96].astype(low)
        send_ref[m, 96:128, :] = extra


def sum_kernel(got_ref, second_ref, table_ref):
    total = got_ref[0].astype(wide)
    for m in range(1, 8):
        total = total + got_ref[m].astype(wide)
    table = total[96:128]
    table_ref[...] = table
    vectors = jnp.concatenate(
        [table[QSLOTS * p + 6 : QSLOTS * p + 8, 0:LANES] for p in range(3)], axis=1
    )
    for a in range(16):
        chunk = jnp.concatenate([total[6 * a : 6 * a + 6], vectors], axis=0)
        second_ref[a] = chunk.astype(low)


def spread_kernel(mine_ref, other_ref, table_ref):
    total = mine_ref[...] + other_ref[...]
    for head in range(HEADS):
        for q in range(6):
            spot = head * QSLOTS + q
            cols = slice(spot // 32 * LANES, (spot // 32 + 1) * LANES)
            width = min(LANES, NBIAS - q * LANES)
            piece = total[spot % 32 : spot % 32 + 1, cols]
            table_ref[head, :, q * LANES : q * LANES + width] = piece[:, 0:width]


def local(
    fields,
    cotangent,
    window_mask,
    mask_token,
    norm_gain,
    qkv_weight,
    out_weight,
    bias_table,
    bias_index,
):
    own_mask = window_mask[:, 0, 0]
    last = (lax.axis_index("lat") == lax.axis_size("lat") - 1).astype(jnp.int32)
    core = lax.axis_index("lon") % 2
    place = jnp.stack([core, last])
    fields = fields.transpose(1, 2, 0, 3)
    cotangent = cotangent.transpose(1, 2, 0, 3)
    smem = pl.BlockSpec(memory_space=pltpu.SMEM)
    vmem = pl.BlockSpec(memory_space=pltpu.VMEM)
    hbm = pl.BlockSpec(memory_space=pltpu.HBM)
    hidden = jnp.repeat(own_mask, 2)[:, None] == 1
    strip = jnp.stack((jnp.where(hidden, jnp.bfloat16(MARK), fields[:3]), cotangent[:3]))
    lat_in = passed_along(strip, "lat", -1)
    bias, order = pl.pallas_call(
        pre_kernel,
        out_shape=(
            jax.ShapeDtypeStruct((HEADS, WIN_TOK, 256), wide),
            jax.ShapeDtypeStruct((D, D), low),
        ),
        in_specs=[smem, hbm, hbm],
        out_specs=(vmem,) * 2,
        scratch_shapes=[
            pltpu.VMEM((HEADS, 1, NBIAS), wide),
            pltpu.VMEM((WIN_TOK, WIN_TOK), jnp.int32),
            pltpu.VMEM((WIN_TOK, LANES), jnp.int32),
            pltpu.VMEM((HEADS * 6, LANES), wide),
            pltpu.SemaphoreType.DMA((2,)),
        ],
        compiler_params=pltpu.CompilerParams(vmem_limit_bytes=8 * 2**20),
        cost_estimate=pl.CostEstimate(flops=5 * 10**9, bytes_accessed=0, transcendentals=0),
    )(place, bias_table.transpose(1, 0, 2), bias_index)
    lat_in, bias, order = lax.optimization_barrier((lat_in, bias, order))
    own = jnp.stack((jnp.where(hidden, jnp.bfloat16(MARK), fields[3:, :6]), cotangent[3:, :6]))
    lon_in = passed_along(jnp.concatenate((own, lat_in[:, :, :6]), axis=1), "lon", -1)

    filled, mixed, igrad, keep, give, bias_grad, bias_tail = pl.pallas_call(
        main_kernel,
        out_shape=(
            jax.ShapeDtypeStruct((TOK, D), low),
            jax.ShapeDtypeStruct((TOK, D), low),
            jax.ShapeDtypeStruct((TOK, D), low),
            jax.ShapeDtypeStruct((8, CHUNK, D), low),
            jax.ShapeDtypeStruct((8, CHUNK, D), low),
            jax.ShapeDtypeStruct((HEADS, WIN_TOK, LANES), wide),
            jax.ShapeDtypeStruct((HEADS, WIN_TOK, LANES), wide),
        ),
        in_specs=[smem, smem] + [vmem] * 6 + [hbm, vmem, vmem, vmem],
        out_specs=(vmem,) * 7,
        scratch_shapes=[
            pltpu.VMEM((TOK, D), wide),
            pltpu.VMEM((TOK, D), wide),
            pltpu.VMEM((TOK, D), wide),
            pltpu.VMEM((TOK, 3 * D), low),
            pltpu.VMEM((TOK, D), low),
            pltpu.VMEM((2, D, WIN_TOK), low),
            pltpu.VMEM((2, D, WIN_TOK), low),
            pltpu.VMEM((TOK, D), low),
            pltpu.VMEM((2, D, WIN_TOK), low),
            pltpu.VMEM((2, D, WIN_TOK), low),
            pltpu.VMEM((3 * D, D), low),
            pltpu.SemaphoreType.DMA(()),
            pltpu.VMEM((3, TOK, LANES), wide),
        ],
        compiler_params=pltpu.CompilerParams(vmem_limit_bytes=24 * 2**20),
        cost_estimate=pl.CostEstimate(
            flops=10**10, bytes_accessed=0, transcendentals=0
        ),
    )(
        place,
        own_mask,
        fields,
        cotangent,
        lat_in,
        lon_in,
        mask_token.astype(wide)[None],
        norm_gain.astype(wide)[None],
        qkv_weight,
        out_weight,
        bias,
        order,
    )

    size = lax.axis_size("lon")

    def swapped(value, bit):
        return lax.ppermute(value, "lon", [(i, i ^ bit) for i in range(size)])

    taken = swapped(give, 1)
    out_own, out_lon = pl.pallas_call(
        out_kernel,
        out_shape=(
            jax.ShapeDtypeStruct((2, 6, 6, 4, D), low),
            jax.ShapeDtypeStruct((2, 6, 6, 4, D), low),
        ),
        in_specs=[vmem] * 4,
        out_specs=(vmem, vmem),
        scratch_shapes=[pltpu.VMEM((3, TOK, LANES), wide)],
        compiler_params=pltpu.CompilerParams(vmem_limit_bytes=16 * 2**20),
        cost_estimate=pl.CostEstimate(flops=2 * 10**9, bytes_accessed=0, transcendentals=0),
    )(filled, mixed, igrad, out_weight)
    lon_out = passed_along(out_lon, "lon", 1)
    bias_grad, out_own = lax.optimization_barrier((bias_grad, out_own))
    table = pl.pallas_call(
        table_kernel,
        out_shape=jax.ShapeDtypeStruct((HEADS * QSLOTS, LANES), wide),
        in_specs=[vmem] * 3,
        out_specs=vmem,
        scratch_shapes=[
            pltpu.VMEM((HEADS, 18, LANES), wide),
            pltpu.VMEM((WIN_TOK, LANES), jnp.int32),
            pltpu.VMEM((WIN_TOK, LANES), jnp.int32),
            pltpu.VMEM((18, LANES), jnp.int32),
        ],
        compiler_params=pltpu.CompilerParams(vmem_limit_bytes=8 * 2**20),
        cost_estimate=pl.CostEstimate(flops=10**9, bytes_accessed=10**6, transcendentals=0),
    )(bias_grad, bias_tail, bias_index)
    pair = pl.pallas_call(
        pack_kernel,
        out_shape=jax.ShapeDtypeStruct((8, 128, D), low),
        in_specs=[vmem] * 3,
        out_specs=vmem,
        compiler_params=pltpu.CompilerParams(vmem_limit_bytes=8 * 2**20),
        cost_estimate=pl.CostEstimate(flops=10**6, bytes_accessed=10**6, transcendentals=0),
    )(keep, taken, table)
    pair, lon_out = lax.optimization_barrier((pair, lon_out))
    groups = [list(range(c, size, 2)) for c in range(2)]
    got = lax.all_to_all(pair, "lon", 0, 0, axis_index_groups=groups, tiled=True)
    second, table = pl.pallas_call(
        sum_kernel,
        out_shape=(
            jax.ShapeDtypeStruct((16, 8, D), low),
            jax.ShapeDtypeStruct((32, D), wide),
        ),
        in_specs=[vmem],
        out_specs=(vmem, vmem),
        compiler_params=pltpu.CompilerParams(vmem_limit_bytes=8 * 2**20),
        cost_estimate=pl.CostEstimate(flops=10**6, bytes_accessed=10**6, transcendentals=0),
    )(got)

    full = jnp.concatenate((lon_out, out_own), axis=2)
    full, second = lax.optimization_barrier((full, second))
    final = lax.all_to_all(second, "lat", 0, 0, tiled=True)
    lat_out = passed_along(full[:, 3:], "lat", 1)
    table_grad = pl.pallas_call(
        spread_kernel,
        out_shape=jax.ShapeDtypeStruct((HEADS, 1, NBIAS), wide),
        in_specs=[vmem, vmem],
        out_specs=vmem,
        cost_estimate=pl.CostEstimate(flops=10**5, bytes_accessed=10**5, transcendentals=0),
    )(table, swapped(table, 1)).transpose(1, 0, 2)
    done = jnp.concatenate((lat_out, full[:, :3]), axis=1).transpose(0, 3, 1, 2, 4)
    output, input_grad = done[0], done[1]
    final, output, input_grad, table_grad = lax.optimization_barrier(
        (final, output, input_grad, table_grad)
    )
    weight_grads = jnp.sum(final[:, :6].astype(wide), axis=0)
    vector_grads = jnp.sum(final[:, 6:].astype(wide), axis=0)
    return (output, input_grad, weight_grads, table_grad, vector_grads)


def solution(mesh):
    placed = (
        P(None, "lat", "lon", None),
        P(None, "lat", "lon", None),
        P(None, "lat", "lon"),
        P(),
        P(),
        P(),
        P(),
        P("lat", None, None),
        P(),
    )
    return jax.shard_map(
        local,
        mesh=mesh,
        in_specs=placed,
        out_specs=(
            P(None, "lat", "lon", None),
            P(None, "lat", "lon", None),
            P(("lat", "lon"), None),
            P("lat", None, None),
            P(),
        ),
        check_vma=False,
    )
```

```python
import functools

import jax
import jax.numpy as jnp
from jax import lax
from jax.experimental import pallas as pl
from jax.experimental.pallas import tpu as pltpu
from jax.sharding import PartitionSpec as P

HEADS = 12
HEAD_DIM = 32
WIN_TOK = 144
NBIAS = 759
D = 384
TOK = 288
EPS = 1e-05
BLOCKED = -10000.0
MARK = 256.0
LANES = 128
LOG2E = 1.4426950408889634
QSLOTS = 8
CHUNK = 104

wide = jnp.float32
low = jnp.bfloat16

NN = (((1,), (0,)), ((), ()))
NT = (((1,), (1,)), ((), ()))
TN = (((0,), (0,)), ((), ()))


def mm(a, b, dims):
    return lax.dot_general(a, b, dims, preferred_element_type=wide)


def passed_along(value, axis, steps):
    count = lax.axis_size(axis)
    pairs = [(source, (source + steps) % count) for source in range(count)]
    return lax.ppermute(value, axis, pairs)


def pre_kernel(
    place_ref, table_in, ids_in, bias_ref, order_ref, table_ref, ids_ref, tail_ref, far_ref, sems
):
    copies = [
        pltpu.make_async_copy(table_in, table_ref, sems.at[0]),
        pltpu.make_async_copy(ids_in, ids_ref, sems.at[1]),
    ]
    for copy in copies:
        copy.start()
    new = lax.broadcasted_iota(jnp.int32, (D, D), 0)
    old = lax.broadcasted_iota(jnp.int32, (D, D), 1)
    tens = new // 6
    r = new - 6 * tens
    a = tens & 3
    j = (tens >> 2) & 7
    other = tens >> 5
    core = place_ref[0]
    c = core + other - 2 * core * other
    order_ref[...] = (old == (a * 16 + 2 * j + c) * 6 + r).astype(wide).astype(low)

    for copy in copies:
        copy.wait()
    tail_ref[...] = jnp.zeros((WIN_TOK, LANES), jnp.int32)
    tail_ref[:, 0:16] = ids_ref[:, LANES:WIN_TOK]
    for head in range(HEADS):
        for p in range(6):
            stop = min((p + 1) * LANES, NBIAS)
            far_ref[head * 6 + p : head * 6 + p + 1, 0 : stop - p * LANES] = (
                table_ref[head, :, p * LANES : stop] * LOG2E
            )

    def rows(step, _):
        at = pl.ds(pl.multiple_of(step * 8, 8), 8)
        for half in range(2):
            ids = ids_ref[at, 0:LANES] if half == 0 else tail_ref[at, :]
            place = ids & (LANES - 1)
            piece = ids >> 7
            picks = [piece == p for p in range(6)]
            for head in range(HEADS):
                got = None
                for p in range(6):
                    source = jnp.broadcast_to(
                        far_ref[head * 6 + p : head * 6 + p + 1, :], (8, LANES)
                    )
                    found = jnp.take_along_axis(source, place, axis=1)
                    got = found if got is None else jnp.where(picks[p], found, got)
                bias_ref[head, at, half * LANES : (half + 1) * LANES] = got
        return 0

    lax.fori_loop(0, WIN_TOK // 8, rows, 0)


def main_kernel(
    place_ref,
    scal_ref,
    fields_ref,
    cot_ref,
    lat_ref,
    lon_ref,
    token_ref,
    gain_ref,
    wqkv_in_ref,
    wout_ref,
    bias_ref,
    order_ref,
    filled_ref,
    mixed_ref,
    igrad_ref,
    keep_ref,
    give_ref,
    bgk_ref,
    bgg_ref,
    x_ref,
    c_ref,
    std_ref,
    qkv_ref,
    gm_ref,
    qt_ref,
    gmt_ref,
    gq_ref,
    gkt_ref,
    gvt_ref,
    bg_ref,
    bt_ref,
    wqkv_ref,
    sem,
    mix_ref,
):
    wqkv_copy = pltpu.make_async_copy(wqkv_in_ref, wqkv_ref, sem)
    wqkv_copy.start()
    level = lax.broadcasted_iota(jnp.int32, (4, 1), 0)
    own_masked = jnp.where(level < 2, scal_ref[0], scal_ref[1]) == 1
    for which, own, dest in ((0, fields_ref, x_ref), (1, cot_ref, c_ref)):
        for a in range(6):
            for o in range(12):
                if o >= 6:
                    piece = lon_ref[which, a, o - 6]
                elif a >= 3:
                    piece = lat_ref[which, a - 3, 6 + o]
                else:
                    piece = own[3 + a, 6 + o]
                piece = piece.astype(wide)
                if which == 0 and o < 6 and a < 3:
                    piece = jnp.where(own_masked, MARK, piece)
                base = (a * 12 + o) * 4
                for c in range(3):
                    mix_ref[c, base : base + 4, :] = piece[:, c * LANES : (c + 1) * LANES]
        for zs in range(4):
            for c in range(3):
                dest[zs * 72 : (zs + 1) * 72, c * LANES : (c + 1) * LANES] = mix_ref[
                    c, pl.ds((zs + 1) % 4, 72, stride=4), :
                ]
    raw = x_ref[...]
    masked = raw > 0.5 * MARK
    filled = jnp.where(masked, token_ref[...], raw)
    filled_ref[...] = filled.astype(low)
    gain = gain_ref[...]
    center = filled - jnp.mean(filled, axis=-1, keepdims=True)
    inv_std = lax.rsqrt(jnp.mean(center * center, axis=-1, keepdims=True) + EPS)
    standard = center * inv_std
    std_ref[...] = standard
    normed = (standard * gain).astype(low)
    cot = c_ref[...].astype(low)

    wqkv_copy.wait()
    qkv_ref[...] = mm(normed, wqkv_ref[...], NT).astype(low)
    gm_ref[...] = mm(cot, wout_ref[...], NN).astype(low)
    for w in range(2):
        rows = slice(w * WIN_TOK, (w + 1) * WIN_TOK)
        qt_ref[w] = mm(wqkv_ref[0:D, :], normed[rows], NT).astype(low)
        gmt_ref[w] = mm(wout_ref[...], cot[rows], (((0,), (1,)), ((), ()))).astype(low)

    last = place_ref[1] == 1
    ti = lax.broadcasted_iota(jnp.int32, (WIN_TOK, WIN_TOK), 0)
    tj = lax.broadcasted_iota(jnp.int32, (WIN_TOK, WIN_TOK), 1)
    zi = (ti >= 72).astype(jnp.int32)
    zj = (tj >= 72).astype(jnp.int32)
    ai = (ti - 72 * zi >= 36).astype(jnp.int32)
    aj = (tj - 72 * zj >= 36).astype(jnp.int32)
    lat_apart = jnp.where(last, (ai != aj).astype(wide), 0.0)
    lev_apart = (zi != zj).astype(wide)
    apart = [
        jnp.concatenate([value] * 4, axis=0) > 0.0 for value in (lat_apart, lat_apart + lev_apart)
    ]
    lane = lax.broadcasted_iota(jnp.int32, (1, LANES), 1) // HEAD_DIM
    scale = HEAD_DIM ** (-0.5)
    masks = [(lane == sub).astype(low) for sub in range(4)]
    for group in range(3):
        cols = slice(group * LANES, (group + 1) * LANES)
        kcols = slice(D + group * LANES, D + (group + 1) * LANES)
        vcols = slice(2 * D + group * LANES, 2 * D + (group + 1) * LANES)
        totals = [None] * 4
        for w in range(2):
            rows = slice(w * WIN_TOK, (w + 1) * WIN_TOK)
            q = qkv_ref[rows, cols]
            k = qkv_ref[rows, kcols]
            v = qkv_ref[rows, vcols]
            g = gm_ref[rows, cols]
            q_four = jnp.concatenate([q * mask for mask in masks], axis=0)
            g_four = jnp.concatenate([g * mask for mask in masks], axis=0)
            biases = jnp.concatenate(
                [bias_ref[group * 4 + sub, :, 0:WIN_TOK] for sub in range(4)], axis=0
            )
            scores = mm(q_four, k, NT) * (scale * LOG2E) + biases
            scores = jnp.where(apart[w], BLOCKED * LOG2E, scores)
            top = jnp.max(scores, axis=-1, keepdims=True)
            expo = jnp.exp2(scores - top)
            prob = (expo * (1.0 / jnp.sum(expo, axis=-1, keepdims=True))).astype(low)
            mixed = mm(prob, v, NN)
            delta = jnp.sum(g_four.astype(wide) * mixed, axis=-1, keepdims=True)
            grad = prob.astype(wide) * (mm(g_four, v, NT) - delta)
            glow = grad.astype(low)
            gq = mm(glow, k, NN)
            mixed_sum = jnp.zeros((WIN_TOK, LANES), wide)
            gq_sum = jnp.zeros((WIN_TOK, LANES), wide)
            for sub in range(4):
                head = group * 4 + sub
                feats = slice(head * HEAD_DIM, (head + 1) * HEAD_DIM)
                part = slice(sub * WIN_TOK, (sub + 1) * WIN_TOK)
                mixed_sum = jnp.where(lane == sub, mixed[part], mixed_sum)
                gq_sum = jnp.where(lane == sub, gq[part], gq_sum)
                gvt_ref[w, feats, :] = mm(gmt_ref[w, feats, :], prob[part], NN).astype(low)
                gkt_ref[w, feats, :] = (mm(qt_ref[w, feats, :], glow[part], NN) * scale).astype(low)
                if w == 0:
                    totals[sub] = grad[part]
                else:
                    total = totals[sub] + grad[part]
                    bg_ref[head] = total[:, 0:LANES]
                    bt_ref[head, :, 0:16] = total[:, LANES:WIN_TOK]
            mixed_ref[rows, cols] = mixed_sum.astype(low)
            gq_ref[rows, cols] = (gq_sum * scale).astype(low)

    mixed = mixed_ref[...]

    core = place_ref[0]
    for i in range(6):
        halves = []
        for head in (i, i + 6):
            tail = [bt_ref[head, pl.ds(k, 18, stride=8), :][:, 0:16] for k in range(8)]
            blank = jnp.zeros((14, LANES), wide)
            halves.append(
                jnp.concatenate([bg_ref[head], jnp.concatenate(tail, axis=1), blank], axis=0)
            )
        bgk_ref[i] = jnp.where(core == 0, halves[0], halves[1])
        bgg_ref[i] = jnp.where(core == 0, halves[1], halves[0]).astype(low)

    gq = gq_ref[...]
    gk = jnp.concatenate([gkt_ref[w].T for w in range(2)], axis=0)
    gv = jnp.concatenate([gvt_ref[w].T for w in range(2)], axis=0)
    grad_normed = (
        mm(gq, wqkv_ref[0:D, :], NN)
        + mm(gk, wqkv_ref[D : 2 * D, :], NN)
        + mm(gv, wqkv_ref[2 * D : 3 * D, :], NN)
    )
    grad_normed = grad_normed.astype(low).astype(wide)
    standard = std_ref[...]
    scaled = grad_normed * gain
    inner = (
        scaled
        - jnp.mean(scaled, axis=-1, keepdims=True)
        - standard * jnp.mean(scaled * standard, axis=-1, keepdims=True)
    )
    grad_filled = c_ref[...] + inv_std * inner
    igrad_ref[...] = jnp.where(masked, 0.0, grad_filled).astype(low)
    gain_grad = jnp.sum(grad_normed * standard, axis=0, keepdims=True)
    token_grad = jnp.sum(jnp.where(masked, grad_filled, 0.0), axis=0, keepdims=True)

    order = order_ref[...]
    parts = []
    for value in (gq, gk, gv, cot):
        turned = mm(order, value, NT).astype(low)
        other = mixed if value is cot else normed
        parts.append(mm(turned, other, NN))
    vectors = jnp.concatenate([gain_grad, token_grad, jnp.zeros((6, D), wide)], axis=0)
    for n in range(16):
        rows = slice(n * 24, (n + 1) * 24)
        chunk = jnp.concatenate([part[rows] for part in parts] + [vectors], axis=0)
        dest = keep_ref if n < 8 else give_ref
        dest[n % 8] = chunk.astype(low)


def out_kernel(filled_ref, mixed_ref, igrad_ref, wout_ref, out_own_ref, out_lon_ref, mix_ref):
    def put_back(which, value):
        for zs in range(4):
            for c in range(3):
                mix_ref[c, pl.ds((zs + 1) % 4, 72, stride=4), :] = value[
                    zs * 72 : (zs + 1) * 72, c * LANES : (c + 1) * LANES
                ]
        for a in range(6):
            for o in range(12):
                base = (a * 12 + o) * 4
                piece = jnp.concatenate([mix_ref[c, base : base + 4, :] for c in range(3)], axis=1)
                if o < 6:
                    out_own_ref[which, a, o] = piece.astype(low)
                else:
                    out_lon_ref[which, a, o - 6] = piece.astype(low)

    branch = mm(mixed_ref[...], wout_ref[...], NT).astype(low).astype(wide)
    put_back(0, filled_ref[...].astype(wide) + branch)
    put_back(1, igrad_ref[...].astype(wide))


def table_kernel(mine_ref, other_ref, ids_ref, sums_ref, total_ref, near_ref, tail_ref, rest_ref):
    slot = lax.broadcasted_iota(jnp.int32, (2 * QSLOTS, LANES), 0)
    slot = jnp.where(slot < QSLOTS, 2 * slot, 2 * (slot - QSLOTS) + 1)
    spot = lax.broadcasted_iota(jnp.int32, (LANES // 2, LANES), 0)
    near_ref[...] = ids_ref[:, 0:LANES]
    tail_ref[:, 0:16] = ids_ref[:, LANES:WIN_TOK]
    rest_ref[...] = jnp.concatenate(
        [tail_ref[pl.ds(k, 18, stride=8), :][:, 0:16] for k in range(8)], axis=1
    )
    total_ref[...] = mine_ref[...] + other_ref[...].astype(wide)

    def one_step(step, acc):
        lefts = []
        rights = []
        for s in range(9):
            if s < 8:
                row = step * 8 + s
                ids = near_ref[pl.ds(row, 1), :]
            else:
                row = WIN_TOK + step
                ids = rest_ref[pl.ds(step, 1), :]
            vals = [total_ref[head, pl.ds(row, 1), :] for head in range(HEADS // 2)]
            rights.append(((ids & (LANES // 2 - 1)) == spot).astype(wide).astype(low))
            here = (ids >> 6) == slot
            lefts.append(
                jnp.concatenate([jnp.where(here, val, 0.0) for val in vals], axis=0).astype(low)
            )
        left = jnp.concatenate(lefts, axis=1)
        right = jnp.concatenate(rights, axis=1)
        return acc + mm(left, right, NT)

    start = jnp.zeros((HEADS * QSLOTS, LANES // 2), wide)
    acc = lax.fori_loop(0, 18, one_step, start, unroll=6)
    for head in range(HEADS // 2):
        even = acc[2 * QSLOTS * head : 2 * QSLOTS * head + QSLOTS]
        odd = acc[2 * QSLOTS * head + QSLOTS : 2 * QSLOTS * (head + 1)]
        sums_ref[QSLOTS * head : QSLOTS * (head + 1), :] = jnp.concatenate([even, odd], axis=1)


def pack_kernel(keep_ref, taken_ref, table_ref, send_ref):
    total = keep_ref[0].astype(wide) + taken_ref[0].astype(wide)
    table = table_ref[...]
    row = lax.broadcasted_iota(jnp.int32, (HEADS // 2 * QSLOTS, 1), 0)
    for n in range(2):
        for p in range(3):
            piece = total[96 + n : 97 + n, p * LANES : (p + 1) * LANES]
            table = jnp.where(row == QSLOTS * p + 6 + n, piece, table)
    extra = jnp.concatenate([table[0:16], table[16:32], table[32:48]], axis=1).astype(low)
    for m in range(8):
        total = keep_ref[m].astype(wide) + taken_ref[m].astype(wide)
        send_ref[m, 0:96, :] = total[0:96].astype(low)
        send_ref[m, 96:112, :] = extra


def sum_kernel(got_ref, second_ref, table_ref):
    total = got_ref[0].astype(wide)
    for m in range(1, 8):
        total = total + got_ref[m].astype(wide)
    extra = total[96:112]
    table = jnp.concatenate([extra[:, p * LANES : (p + 1) * LANES] for p in range(3)], axis=0)
    table_ref[...] = table
    vectors = jnp.concatenate(
        [table[QSLOTS * p + 6 : QSLOTS * p + 8] for p in range(3)], axis=1
    )
    for a in range(16):
        chunk = jnp.concatenate([total[6 * a : 6 * a + 6], vectors], axis=0)
        second_ref[a] = chunk.astype(low)


def spread_kernel(place_ref, mine_ref, other_ref, table_ref):
    mine = mine_ref[...]
    other = other_ref[...]
    halves = (
        jnp.where(place_ref[0] == 0, mine, other),
        jnp.where(place_ref[0] == 0, other, mine),
    )
    for head in range(HEADS):
        for q in range(6):
            spot = head % 6 * QSLOTS + q
            width = min(LANES, NBIAS - q * LANES)
            piece = halves[head // 6][spot : spot + 1, :]
            table_ref[head, :, q * LANES : q * LANES + width] = piece[:, 0:width]


def local(
    fields,
    cotangent,
    window_mask,
    mask_token,
    norm_gain,
    qkv_weight,
    out_weight,
    bias_table,
    bias_index,
):
    own_mask = window_mask[:, 0, 0]
    last = (lax.axis_index("lat") == lax.axis_size("lat") - 1).astype(jnp.int32)
    core = lax.axis_index("lon") % 2
    place = jnp.stack([core, last])
    fields = fields.transpose(1, 2, 0, 3)
    cotangent = cotangent.transpose(1, 2, 0, 3)
    smem = pl.BlockSpec(memory_space=pltpu.SMEM)
    vmem = pl.BlockSpec(memory_space=pltpu.VMEM)
    hbm = pl.BlockSpec(memory_space=pltpu.HBM)
    hidden = jnp.repeat(own_mask, 2)[:, None] == 1
    strip = jnp.stack((jnp.where(hidden, jnp.bfloat16(MARK), fields[:3]), cotangent[:3]))
    lat_in = passed_along(strip, "lat", -1)
    bias, order = pl.pallas_call(
        pre_kernel,
        out_shape=(
            jax.ShapeDtypeStruct((HEADS, WIN_TOK, 256), wide),
            jax.ShapeDtypeStruct((D, D), low),
        ),
        in_specs=[smem, hbm, hbm],
        out_specs=(vmem,) * 2,
        scratch_shapes=[
            pltpu.VMEM((HEADS, 1, NBIAS), wide),
            pltpu.VMEM((WIN_TOK, WIN_TOK), jnp.int32),
            pltpu.VMEM((WIN_TOK, LANES), jnp.int32),
            pltpu.VMEM((HEADS * 6, LANES), wide),
            pltpu.SemaphoreType.DMA((2,)),
        ],
        compiler_params=pltpu.CompilerParams(vmem_limit_bytes=8 * 2**20),
        cost_estimate=pl.CostEstimate(flops=5 * 10**9, bytes_accessed=0, transcendentals=0),
    )(place, bias_table.transpose(1, 0, 2), bias_index)
    lat_in, bias, order = lax.optimization_barrier((lat_in, bias, order))
    own = jnp.stack((jnp.where(hidden, jnp.bfloat16(MARK), fields[3:, :6]), cotangent[3:, :6]))
    lon_in = passed_along(jnp.concatenate((own, lat_in[:, :, :6]), axis=1), "lon", -1)

    filled, mixed, igrad, keep, give, pairs, pairs_give = pl.pallas_call(
        main_kernel,
        out_shape=(
            jax.ShapeDtypeStruct((TOK, D), low),
            jax.ShapeDtypeStruct((TOK, D), low),
            jax.ShapeDtypeStruct((TOK, D), low),
            jax.ShapeDtypeStruct((8, CHUNK, D), low),
            jax.ShapeDtypeStruct((8, CHUNK, D), low),
            jax.ShapeDtypeStruct((HEADS // 2, 176, LANES), wide),
            jax.ShapeDtypeStruct((HEADS // 2, 176, LANES), low),
        ),
        in_specs=[smem, smem] + [vmem] * 6 + [hbm, vmem, vmem, vmem],
        out_specs=(vmem,) * 7,
        scratch_shapes=[
            pltpu.VMEM((TOK, D), wide),
            pltpu.VMEM((TOK, D), wide),
            pltpu.VMEM((TOK, D), wide),
            pltpu.VMEM((TOK, 3 * D), low),
            pltpu.VMEM((TOK, D), low),
            pltpu.VMEM((2, D, WIN_TOK), low),
            pltpu.VMEM((2, D, WIN_TOK), low),
            pltpu.VMEM((TOK, D), low),
            pltpu.VMEM((2, D, WIN_TOK), low),
            pltpu.VMEM((2, D, WIN_TOK), low),
            pltpu.VMEM((HEADS, WIN_TOK, LANES), wide),
            pltpu.VMEM((HEADS, WIN_TOK, LANES), wide),
            pltpu.VMEM((3 * D, D), low),
            pltpu.SemaphoreType.DMA(()),
            pltpu.VMEM((3, TOK, LANES), wide),
        ],
        compiler_params=pltpu.CompilerParams(vmem_limit_bytes=24 * 2**20),
        cost_estimate=pl.CostEstimate(
            flops=10**10, bytes_accessed=0, transcendentals=0
        ),
    )(
        place,
        own_mask,
        fields,
        cotangent,
        lat_in,
        lon_in,
        mask_token.astype(wide)[None],
        norm_gain.astype(wide)[None],
        qkv_weight,
        out_weight,
        bias,
        order,
    )

    size = lax.axis_size("lon")

    def swapped(value, bit):
        return lax.ppermute(value, "lon", [(i, i ^ bit) for i in range(size)])

    out_own, out_lon = pl.pallas_call(
        out_kernel,
        out_shape=(
            jax.ShapeDtypeStruct((2, 6, 6, 4, D), low),
            jax.ShapeDtypeStruct((2, 6, 6, 4, D), low),
        ),
        in_specs=[vmem] * 4,
        out_specs=(vmem, vmem),
        scratch_shapes=[pltpu.VMEM((3, TOK, LANES), wide)],
        compiler_params=pltpu.CompilerParams(vmem_limit_bytes=16 * 2**20),
        cost_estimate=pl.CostEstimate(flops=2 * 10**9, bytes_accessed=0, transcendentals=0),
    )(filled, mixed, igrad, out_weight)
    lon_out = passed_along(out_lon, "lon", 1)
    give, pairs_give, out_own = lax.optimization_barrier((give, pairs_give, out_own))
    other_pairs = swapped(pairs_give, 1)
    taken = swapped(give, 1)
    table = pl.pallas_call(
        table_kernel,
        out_shape=jax.ShapeDtypeStruct((HEADS // 2 * QSLOTS, LANES), wide),
        in_specs=[vmem] * 3,
        out_specs=vmem,
        scratch_shapes=[
            pltpu.VMEM((HEADS // 2, 176, LANES), wide),
            pltpu.VMEM((WIN_TOK, LANES), jnp.int32),
            pltpu.VMEM((WIN_TOK, LANES), jnp.int32),
            pltpu.VMEM((18, LANES), jnp.int32),
        ],
        compiler_params=pltpu.CompilerParams(vmem_limit_bytes=8 * 2**20),
        cost_estimate=pl.CostEstimate(flops=10**9, bytes_accessed=10**6, transcendentals=0),
    )(pairs, other_pairs, bias_index)
    pair = pl.pallas_call(
        pack_kernel,
        out_shape=jax.ShapeDtypeStruct((8, 112, D), low),
        in_specs=[vmem] * 3,
        out_specs=vmem,
        compiler_params=pltpu.CompilerParams(vmem_limit_bytes=8 * 2**20),
        cost_estimate=pl.CostEstimate(flops=10**6, bytes_accessed=10**6, transcendentals=0),
    )(keep, taken, table)
    pair, lon_out = lax.optimization_barrier((pair, lon_out))
    groups = [list(range(c, size, 2)) for c in range(2)]
    got = lax.all_to_all(pair, "lon", 0, 0, axis_index_groups=groups, tiled=True)
    second, table = pl.pallas_call(
        sum_kernel,
        out_shape=(
            jax.ShapeDtypeStruct((16, 8, D), low),
            jax.ShapeDtypeStruct((HEADS // 2 * QSLOTS, LANES), wide),
        ),
        in_specs=[vmem],
        out_specs=(vmem, vmem),
        compiler_params=pltpu.CompilerParams(vmem_limit_bytes=8 * 2**20),
        cost_estimate=pl.CostEstimate(flops=10**6, bytes_accessed=10**6, transcendentals=0),
    )(got)

    full = jnp.concatenate((lon_out, out_own), axis=2)
    full, second = lax.optimization_barrier((full, second))
    final = lax.all_to_all(second, "lat", 0, 0, tiled=True)
    lat_out = passed_along(full[:, 3:], "lat", 1)
    table, _ = lax.optimization_barrier((table, lat_out))
    table_grad = pl.pallas_call(
        spread_kernel,
        out_shape=jax.ShapeDtypeStruct((HEADS, 1, NBIAS), wide),
        in_specs=[smem, vmem, vmem],
        out_specs=vmem,
        cost_estimate=pl.CostEstimate(flops=10**5, bytes_accessed=10**5, transcendentals=0),
    )(place, table, swapped(table, 1)).transpose(1, 0, 2)
    done = jnp.concatenate((lat_out, full[:, :3]), axis=1).transpose(0, 3, 1, 2, 4)
    output, input_grad = done[0], done[1]
    final, output, input_grad, table_grad = lax.optimization_barrier(
        (final, output, input_grad, table_grad)
    )
    weight_grads = jnp.sum(final[:, :6].astype(wide), axis=0)
    vector_grads = jnp.sum(final[:, 6:].astype(wide), axis=0)
    return (output, input_grad, weight_grads, table_grad, vector_grads)


def solution(mesh):
    placed = (
        P(None, "lat", "lon", None),
        P(None, "lat", "lon", None),
        P(None, "lat", "lon"),
        P(),
        P(),
        P(),
        P(),
        P("lat", None, None),
        P(),
    )
    return jax.shard_map(
        local,
        mesh=mesh,
        in_specs=placed,
        out_specs=(
            P(None, "lat", "lon", None),
            P(None, "lat", "lon", None),
            P(("lat", "lon"), None),
            P("lat", None, None),
            P(),
        ),
        check_vma=False,
    )
```

```python
import functools

import jax
import jax.numpy as jnp
from jax import lax
from jax.experimental import pallas as pl
from jax.experimental.pallas import tpu as pltpu
from jax.sharding import PartitionSpec as P

HEADS = 12
HEAD_DIM = 32
WIN_TOK = 144
NBIAS = 759
D = 384
TOK = 288
EPS = 1e-05
BLOCKED = -10000.0
MARK = 256.0
LANES = 128
LOG2E = 1.4426950408889634
QSLOTS = 8
CHUNK = 104

wide = jnp.float32
low = jnp.bfloat16

NN = (((1,), (0,)), ((), ()))
NT = (((1,), (1,)), ((), ()))
TN = (((0,), (0,)), ((), ()))


def mm(a, b, dims):
    return lax.dot_general(a, b, dims, preferred_element_type=wide)


def passed_along(value, axis, steps):
    count = lax.axis_size(axis)
    pairs = [(source, (source + steps) % count) for source in range(count)]
    return lax.ppermute(value, axis, pairs)


def pre_kernel(
    place_ref, table_in, ids_in, bias_ref, order_ref, table_ref, ids_ref, tail_ref, far_ref, sems
):
    copies = [
        pltpu.make_async_copy(table_in, table_ref, sems.at[0]),
        pltpu.make_async_copy(ids_in, ids_ref, sems.at[1]),
    ]
    for copy in copies:
        copy.start()
    new = lax.broadcasted_iota(jnp.int32, (D, D), 0)
    old = lax.broadcasted_iota(jnp.int32, (D, D), 1)
    tens = new // 6
    r = new - 6 * tens
    a = tens & 3
    j = (tens >> 2) & 7
    other = tens >> 5
    core = place_ref[0]
    c = core + other - 2 * core * other
    order_ref[...] = (old == (a * 16 + 2 * j + c) * 6 + r).astype(wide).astype(low)

    for copy in copies:
        copy.wait()
    tail_ref[...] = jnp.zeros((WIN_TOK, LANES), jnp.int32)
    tail_ref[:, 0:16] = ids_ref[:, LANES:WIN_TOK]
    for head in range(HEADS):
        for p in range(6):
            stop = min((p + 1) * LANES, NBIAS)
            far_ref[head * 6 + p : head * 6 + p + 1, 0 : stop - p * LANES] = (
                table_ref[head, :, p * LANES : stop] * LOG2E
            )

    def rows(step, _):
        at = pl.ds(pl.multiple_of(step * 8, 8), 8)
        for half in range(2):
            ids = ids_ref[at, 0:LANES] if half == 0 else tail_ref[at, :]
            place = ids & (LANES - 1)
            piece = ids >> 7
            picks = [piece == p for p in range(6)]
            for head in range(HEADS):
                got = None
                for p in range(6):
                    source = jnp.broadcast_to(
                        far_ref[head * 6 + p : head * 6 + p + 1, :], (8, LANES)
                    )
                    found = jnp.take_along_axis(source, place, axis=1)
                    got = found if got is None else jnp.where(picks[p], found, got)
                bias_ref[head, at, half * LANES : (half + 1) * LANES] = got
        return 0

    lax.fori_loop(0, WIN_TOK // 8, rows, 0)


def main_kernel(
    place_ref,
    scal_ref,
    fields_ref,
    cot_ref,
    lat_ref,
    lon_ref,
    token_ref,
    gain_ref,
    wqkv_in_ref,
    wout_ref,
    bias_ref,
    order_ref,
    filled_ref,
    mixed_ref,
    igrad_ref,
    keep_ref,
    give_ref,
    bgk_ref,
    bgg_ref,
    x_ref,
    c_ref,
    std_ref,
    qkv_ref,
    gm_ref,
    qt_ref,
    gmt_ref,
    gq_ref,
    gkt_ref,
    gvt_ref,
    bg_ref,
    bt_ref,
    wqkv_ref,
    sem,
    mix_ref,
):
    wqkv_copy = pltpu.make_async_copy(wqkv_in_ref, wqkv_ref, sem)
    wqkv_copy.start()
    level = lax.broadcasted_iota(jnp.int32, (4, 1), 0)
    own_masked = jnp.where(level < 2, scal_ref[0], scal_ref[1]) == 1
    for which, own, dest in ((0, fields_ref, x_ref), (1, cot_ref, c_ref)):
        for a in range(6):
            for o in range(12):
                if o >= 6:
                    piece = lon_ref[which, a, o - 6]
                elif a >= 3:
                    piece = lat_ref[which, a - 3, 6 + o]
                else:
                    piece = own[3 + a, 6 + o]
                piece = piece.astype(wide)
                if which == 0 and o < 6 and a < 3:
                    piece = jnp.where(own_masked, MARK, piece)
                base = (a * 12 + o) * 4
                for c in range(3):
                    mix_ref[c, base : base + 4, :] = piece[:, c * LANES : (c + 1) * LANES]
        for zs in range(4):
            for c in range(3):
                dest[zs * 72 : (zs + 1) * 72, c * LANES : (c + 1) * LANES] = mix_ref[
                    c, pl.ds((zs + 1) % 4, 72, stride=4), :
                ]
    raw = x_ref[...]
    masked = raw > 0.5 * MARK
    filled = jnp.where(masked, token_ref[...], raw)
    filled_ref[...] = filled.astype(low)
    gain = gain_ref[...]
    center = filled - jnp.mean(filled, axis=-1, keepdims=True)
    inv_std = lax.rsqrt(jnp.mean(center * center, axis=-1, keepdims=True) + EPS)
    standard = center * inv_std
    std_ref[...] = standard
    normed = (standard * gain).astype(low)
    cot = c_ref[...].astype(low)

    wqkv_copy.wait()
    qkv_ref[...] = mm(normed, wqkv_ref[...], NT).astype(low)
    gm_ref[...] = mm(cot, wout_ref[...], NN).astype(low)
    for w in range(2):
        rows = slice(w * WIN_TOK, (w + 1) * WIN_TOK)
        qt_ref[w] = mm(wqkv_ref[0:D, :], normed[rows], NT).astype(low)
        gmt_ref[w] = mm(wout_ref[...], cot[rows], (((0,), (1,)), ((), ()))).astype(low)

    last = place_ref[1] == 1
    ti = lax.broadcasted_iota(jnp.int32, (WIN_TOK, WIN_TOK), 0)
    tj = lax.broadcasted_iota(jnp.int32, (WIN_TOK, WIN_TOK), 1)
    zi = (ti >= 72).astype(jnp.int32)
    zj = (tj >= 72).astype(jnp.int32)
    ai = (ti - 72 * zi >= 36).astype(jnp.int32)
    aj = (tj - 72 * zj >= 36).astype(jnp.int32)
    lat_apart = jnp.where(last, (ai != aj).astype(wide), 0.0)
    lev_apart = (zi != zj).astype(wide)
    apart = [
        jnp.concatenate([value] * 4, axis=0) > 0.0 for value in (lat_apart, lat_apart + lev_apart)
    ]
    lane = lax.broadcasted_iota(jnp.int32, (1, LANES), 1) // HEAD_DIM
    scale = HEAD_DIM ** (-0.5)
    masks = [(lane == sub).astype(low) for sub in range(4)]
    totals = [None] * HEADS

    def first_products(group, w):
        rows = slice(w * WIN_TOK, (w + 1) * WIN_TOK)
        q = qkv_ref[rows, group * LANES : (group + 1) * LANES]
        k = qkv_ref[rows, D + group * LANES : D + (group + 1) * LANES]
        v = qkv_ref[rows, 2 * D + group * LANES : 2 * D + (group + 1) * LANES]
        g = gm_ref[rows, group * LANES : (group + 1) * LANES]
        g_four = jnp.concatenate([g * mask for mask in masks], axis=0)
        scores = mm(jnp.concatenate([q * mask for mask in masks], axis=0), k, NT)
        return k, v, g_four, scores, mm(g_four, v, NT)

    def weights_of(group, w, k, v, g_four, scores, grad_attn):
        biases = jnp.concatenate(
            [bias_ref[group * 4 + sub, :, 0:WIN_TOK] for sub in range(4)], axis=0
        )
        scores = scores * (scale * LOG2E) + biases
        scores = jnp.where(apart[w], BLOCKED * LOG2E, scores)
        top = jnp.max(scores, axis=-1, keepdims=True)
        expo = jnp.exp2(scores - top)
        prob = (expo * (1.0 / jnp.sum(expo, axis=-1, keepdims=True))).astype(low)
        return k, g_four, grad_attn, prob, mm(prob, v, NN)

    def score_grads(group, w, k, g_four, grad_attn, prob, mixed):
        delta = jnp.sum(g_four.astype(wide) * mixed, axis=-1, keepdims=True)
        grad = prob.astype(wide) * (grad_attn - delta)
        for sub in range(4):
            head = group * 4 + sub
            part = slice(sub * WIN_TOK, (sub + 1) * WIN_TOK)
            if w == 0:
                totals[head] = grad[part]
            else:
                total = totals[head] + grad[part]
                bg_ref[head] = total[:, 0:LANES]
                bt_ref[head, :, 0:16] = total[:, LANES:WIN_TOK]
        return k, prob, mixed, grad.astype(low)

    def last_products(group, w, k, prob, mixed, glow):
        cols = slice(group * LANES, (group + 1) * LANES)
        rows = slice(w * WIN_TOK, (w + 1) * WIN_TOK)
        gq = mm(glow, k, NN)
        mixed_sum = jnp.zeros((WIN_TOK, LANES), wide)
        gq_sum = jnp.zeros((WIN_TOK, LANES), wide)
        for sub in range(4):
            head = group * 4 + sub
            feats = slice(head * HEAD_DIM, (head + 1) * HEAD_DIM)
            part = slice(sub * WIN_TOK, (sub + 1) * WIN_TOK)
            mixed_sum = jnp.where(lane == sub, mixed[part], mixed_sum)
            gq_sum = jnp.where(lane == sub, gq[part], gq_sum)
            gvt_ref[w, feats, :] = mm(gmt_ref[w, feats, :], prob[part], NN).astype(low)
            gkt_ref[w, feats, :] = (mm(qt_ref[w, feats, :], glow[part], NN) * scale).astype(low)
        mixed_ref[rows, cols] = mixed_sum.astype(low)
        gq_ref[rows, cols] = (gq_sum * scale).astype(low)

    work = [(group, w) for group in range(3) for w in range(2)]
    states = [None] * 6
    for n in range(-3, 9):
        if 0 <= n + 1 < 6:
            states[n + 1] = first_products(*work[n + 1])
        if 0 <= n < 6:
            states[n] = weights_of(*work[n], *states[n])
        if 0 <= n - 1 < 6:
            last_products(*work[n - 1], *states[n - 1])
        if 0 <= n < 6:
            states[n] = score_grads(*work[n], *states[n])

    mixed = mixed_ref[...]

    core = place_ref[0]
    for i in range(6):
        halves = []
        for head in (i, i + 6):
            tail = [bt_ref[head, pl.ds(k, 18, stride=8), :][:, 0:16] for k in range(8)]
            blank = jnp.zeros((14, LANES), wide)
            halves.append(
                jnp.concatenate([bg_ref[head], jnp.concatenate(tail, axis=1), blank], axis=0)
            )
        bgk_ref[i] = jnp.where(core == 0, halves[0], halves[1])
        bgg_ref[i] = jnp.where(core == 0, halves[1], halves[0]).astype(low)

    gq = gq_ref[...]
    gk = jnp.concatenate([gkt_ref[w].T for w in range(2)], axis=0)
    gv = jnp.concatenate([gvt_ref[w].T for w in range(2)], axis=0)
    grad_normed = (
        mm(gq, wqkv_ref[0:D, :], NN)
        + mm(gk, wqkv_ref[D : 2 * D, :], NN)
        + mm(gv, wqkv_ref[2 * D : 3 * D, :], NN)
    )
    grad_normed = grad_normed.astype(low).astype(wide)
    standard = std_ref[...]
    scaled = grad_normed * gain
    inner = (
        scaled
        - jnp.mean(scaled, axis=-1, keepdims=True)
        - standard * jnp.mean(scaled * standard, axis=-1, keepdims=True)
    )
    grad_filled = c_ref[...] + inv_std * inner
    igrad_ref[...] = jnp.where(masked, 0.0, grad_filled).astype(low)
    gain_grad = jnp.sum(grad_normed * standard, axis=0, keepdims=True)
    token_grad = jnp.sum(jnp.where(masked, grad_filled, 0.0), axis=0, keepdims=True)

    order = order_ref[...]
    turned = [mm(order, value, NT).astype(low) for value in (gq, gk, gv, cot)]
    parts = [mm(value, normed, NN) for value in turned[:3]] + [mm(turned[3], mixed, NN)]
    vectors = jnp.concatenate([gain_grad, token_grad, jnp.zeros((6, D), wide)], axis=0)
    for n in range(16):
        rows = slice(n * 24, (n + 1) * 24)
        chunk = jnp.concatenate([part[rows] for part in parts] + [vectors], axis=0)
        dest = keep_ref if n < 8 else give_ref
        dest[n % 8] = chunk.astype(low)


def out_kernel(filled_ref, mixed_ref, igrad_ref, wout_ref, out_own_ref, out_lon_ref, mix_ref):
    def put_back(which, value):
        for zs in range(4):
            for c in range(3):
                mix_ref[c, pl.ds((zs + 1) % 4, 72, stride=4), :] = value[
                    zs * 72 : (zs + 1) * 72, c * LANES : (c + 1) * LANES
                ]
        for a in range(6):
            for o in range(12):
                base = (a * 12 + o) * 4
                piece = jnp.concatenate([mix_ref[c, base : base + 4, :] for c in range(3)], axis=1)
                if o < 6:
                    out_own_ref[which, a, o] = piece.astype(low)
                else:
                    out_lon_ref[which, a, o - 6] = piece.astype(low)

    branch = mm(mixed_ref[...], wout_ref[...], NT).astype(low).astype(wide)
    put_back(0, filled_ref[...].astype(wide) + branch)
    put_back(1, igrad_ref[...].astype(wide))


def table_kernel(mine_ref, other_ref, ids_ref, sums_ref, total_ref, near_ref, tail_ref, rest_ref):
    slot = lax.broadcasted_iota(jnp.int32, (2 * QSLOTS, LANES), 0)
    slot = jnp.where(slot < QSLOTS, 2 * slot, 2 * (slot - QSLOTS) + 1)
    spot = lax.broadcasted_iota(jnp.int32, (LANES // 2, LANES), 0)
    near_ref[...] = ids_ref[:, 0:LANES]
    tail_ref[:, 0:16] = ids_ref[:, LANES:WIN_TOK]
    rest_ref[...] = jnp.concatenate(
        [tail_ref[pl.ds(k, 18, stride=8), :][:, 0:16] for k in range(8)], axis=1
    )
    total_ref[...] = mine_ref[...] + other_ref[...].astype(wide)

    def one_step(step, acc):
        lefts = []
        rights = []
        for s in range(9):
            if s < 8:
                row = step * 8 + s
                ids = near_ref[pl.ds(row, 1), :]
            else:
                row = WIN_TOK + step
                ids = rest_ref[pl.ds(step, 1), :]
            vals = [total_ref[head, pl.ds(row, 1), :] for head in range(HEADS // 2)]
            rights.append(((ids & (LANES // 2 - 1)) == spot).astype(wide).astype(low))
            here = (ids >> 6) == slot
            lefts.append(
                jnp.concatenate([jnp.where(here, val, 0.0) for val in vals], axis=0).astype(low)
            )
        left = jnp.concatenate(lefts, axis=1)
        right = jnp.concatenate(rights, axis=1)
        return acc + mm(left, right, NT)

    start = jnp.zeros((HEADS * QSLOTS, LANES // 2), wide)
    acc = lax.fori_loop(0, 18, one_step, start, unroll=6)
    for head in range(HEADS // 2):
        even = acc[2 * QSLOTS * head : 2 * QSLOTS * head + QSLOTS]
        odd = acc[2 * QSLOTS * head + QSLOTS : 2 * QSLOTS * (head + 1)]
        sums_ref[QSLOTS * head : QSLOTS * (head + 1), :] = jnp.concatenate([even, odd], axis=1)


def pack_kernel(keep_ref, taken_ref, table_ref, send_ref):
    total = keep_ref[0].astype(wide) + taken_ref[0].astype(wide)
    table = table_ref[...]
    row = lax.broadcasted_iota(jnp.int32, (HEADS // 2 * QSLOTS, 1), 0)
    for n in range(2):
        for p in range(3):
            piece = total[96 + n : 97 + n, p * LANES : (p + 1) * LANES]
            table = jnp.where(row == QSLOTS * p + 6 + n, piece, table)
    extra = jnp.concatenate([table[0:16], table[16:32], table[32:48]], axis=1).astype(low)
    for m in range(8):
        total = keep_ref[m].astype(wide) + taken_ref[m].astype(wide)
        send_ref[m, 0:96, :] = total[0:96].astype(low)
        send_ref[m, 96:112, :] = extra


def sum_kernel(got_ref, second_ref, table_ref):
    total = got_ref[0].astype(wide)
    for m in range(1, 8):
        total = total + got_ref[m].astype(wide)
    extra = total[96:112]
    table = jnp.concatenate([extra[:, p * LANES : (p + 1) * LANES] for p in range(3)], axis=0)
    table_ref[...] = table
    vectors = jnp.concatenate(
        [table[QSLOTS * p + 6 : QSLOTS * p + 8] for p in range(3)], axis=1
    )
    for a in range(16):
        chunk = jnp.concatenate([total[6 * a : 6 * a + 6], vectors], axis=0)
        second_ref[a] = chunk.astype(low)


def spread_kernel(place_ref, mine_ref, other_ref, table_ref):
    mine = mine_ref[...]
    other = other_ref[...]
    halves = (
        jnp.where(place_ref[0] == 0, mine, other),
        jnp.where(place_ref[0] == 0, other, mine),
    )
    for head in range(HEADS):
        for q in range(6):
            spot = head % 6 * QSLOTS + q
            width = min(LANES, NBIAS - q * LANES)
            piece = halves[head // 6][spot : spot + 1, :]
            table_ref[head, :, q * LANES : q * LANES + width] = piece[:, 0:width]


def local(
    fields,
    cotangent,
    window_mask,
    mask_token,
    norm_gain,
    qkv_weight,
    out_weight,
    bias_table,
    bias_index,
):
    own_mask = window_mask[:, 0, 0]
    last = (lax.axis_index("lat") == lax.axis_size("lat") - 1).astype(jnp.int32)
    core = lax.axis_index("lon") % 2
    place = jnp.stack([core, last])
    fields = fields.transpose(1, 2, 0, 3)
    cotangent = cotangent.transpose(1, 2, 0, 3)
    smem = pl.BlockSpec(memory_space=pltpu.SMEM)
    vmem = pl.BlockSpec(memory_space=pltpu.VMEM)
    hbm = pl.BlockSpec(memory_space=pltpu.HBM)
    hidden = jnp.repeat(own_mask, 2)[:, None] == 1
    strip = jnp.stack((jnp.where(hidden, jnp.bfloat16(MARK), fields[:3]), cotangent[:3]))
    lat_in = passed_along(strip, "lat", -1)
    bias, order = pl.pallas_call(
        pre_kernel,
        out_shape=(
            jax.ShapeDtypeStruct((HEADS, WIN_TOK, 256), wide),
            jax.ShapeDtypeStruct((D, D), low),
        ),
        in_specs=[smem, hbm, hbm],
        out_specs=(vmem,) * 2,
        scratch_shapes=[
            pltpu.VMEM((HEADS, 1, NBIAS), wide),
            pltpu.VMEM((WIN_TOK, WIN_TOK), jnp.int32),
            pltpu.VMEM((WIN_TOK, LANES), jnp.int32),
            pltpu.VMEM((HEADS * 6, LANES), wide),
            pltpu.SemaphoreType.DMA((2,)),
        ],
        compiler_params=pltpu.CompilerParams(vmem_limit_bytes=8 * 2**20),
        cost_estimate=pl.CostEstimate(flops=5 * 10**9, bytes_accessed=0, transcendentals=0),
    )(place, bias_table.transpose(1, 0, 2), bias_index)
    lat_in, bias, order = lax.optimization_barrier((lat_in, bias, order))
    own = jnp.stack((jnp.where(hidden, jnp.bfloat16(MARK), fields[3:, :6]), cotangent[3:, :6]))
    lon_in = passed_along(jnp.concatenate((own, lat_in[:, :, :6]), axis=1), "lon", -1)

    filled, mixed, igrad, keep, give, pairs, pairs_give = pl.pallas_call(
        main_kernel,
        out_shape=(
            jax.ShapeDtypeStruct((TOK, D), low),
            jax.ShapeDtypeStruct((TOK, D), low),
            jax.ShapeDtypeStruct((TOK, D), low),
            jax.ShapeDtypeStruct((8, CHUNK, D), low),
            jax.ShapeDtypeStruct((8, CHUNK, D), low),
            jax.ShapeDtypeStruct((HEADS // 2, 176, LANES), wide),
            jax.ShapeDtypeStruct((HEADS // 2, 176, LANES), low),
        ),
        in_specs=[smem, smem] + [vmem] * 6 + [hbm, vmem, vmem, vmem],
        out_specs=(vmem,) * 7,
        scratch_shapes=[
            pltpu.VMEM((TOK, D), wide),
            pltpu.VMEM((TOK, D), wide),
            pltpu.VMEM((TOK, D), wide),
            pltpu.VMEM((TOK, 3 * D), low),
            pltpu.VMEM((TOK, D), low),
            pltpu.VMEM((2, D, WIN_TOK), low),
            pltpu.VMEM((2, D, WIN_TOK), low),
            pltpu.VMEM((TOK, D), low),
            pltpu.VMEM((2, D, WIN_TOK), low),
            pltpu.VMEM((2, D, WIN_TOK), low),
            pltpu.VMEM((HEADS, WIN_TOK, LANES), wide),
            pltpu.VMEM((HEADS, WIN_TOK, LANES), wide),
            pltpu.VMEM((3 * D, D), low),
            pltpu.SemaphoreType.DMA(()),
            pltpu.VMEM((3, TOK, LANES), wide),
        ],
        compiler_params=pltpu.CompilerParams(vmem_limit_bytes=24 * 2**20),
        cost_estimate=pl.CostEstimate(
            flops=10**10, bytes_accessed=0, transcendentals=0
        ),
    )(
        place,
        own_mask,
        fields,
        cotangent,
        lat_in,
        lon_in,
        mask_token.astype(wide)[None],
        norm_gain.astype(wide)[None],
        qkv_weight,
        out_weight,
        bias,
        order,
    )

    size = lax.axis_size("lon")

    def swapped(value, bit):
        return lax.ppermute(value, "lon", [(i, i ^ bit) for i in range(size)])

    out_own, out_lon = pl.pallas_call(
        out_kernel,
        out_shape=(
            jax.ShapeDtypeStruct((2, 6, 6, 4, D), low),
            jax.ShapeDtypeStruct((2, 6, 6, 4, D), low),
        ),
        in_specs=[vmem] * 4,
        out_specs=(vmem, vmem),
        scratch_shapes=[pltpu.VMEM((3, TOK, LANES), wide)],
        compiler_params=pltpu.CompilerParams(vmem_limit_bytes=16 * 2**20),
        cost_estimate=pl.CostEstimate(flops=2 * 10**9, bytes_accessed=0, transcendentals=0),
    )(filled, mixed, igrad, out_weight)
    lon_out = passed_along(out_lon, "lon", 1)
    give, pairs_give, out_own = lax.optimization_barrier((give, pairs_give, out_own))
    other_pairs = swapped(pairs_give, 1)
    taken = swapped(give, 1)
    table = pl.pallas_call(
        table_kernel,
        out_shape=jax.ShapeDtypeStruct((HEADS // 2 * QSLOTS, LANES), wide),
        in_specs=[vmem] * 3,
        out_specs=vmem,
        scratch_shapes=[
            pltpu.VMEM((HEADS // 2, 176, LANES), wide),
            pltpu.VMEM((WIN_TOK, LANES), jnp.int32),
            pltpu.VMEM((WIN_TOK, LANES), jnp.int32),
            pltpu.VMEM((18, LANES), jnp.int32),
        ],
        compiler_params=pltpu.CompilerParams(vmem_limit_bytes=8 * 2**20),
        cost_estimate=pl.CostEstimate(flops=10**9, bytes_accessed=10**6, transcendentals=0),
    )(pairs, other_pairs, bias_index)
    pair = pl.pallas_call(
        pack_kernel,
        out_shape=jax.ShapeDtypeStruct((8, 112, D), low),
        in_specs=[vmem] * 3,
        out_specs=vmem,
        compiler_params=pltpu.CompilerParams(vmem_limit_bytes=8 * 2**20),
        cost_estimate=pl.CostEstimate(flops=10**6, bytes_accessed=10**6, transcendentals=0),
    )(keep, taken, table)
    pair, lon_out = lax.optimization_barrier((pair, lon_out))
    groups = [list(range(c, size, 2)) for c in range(2)]
    got = lax.all_to_all(pair, "lon", 0, 0, axis_index_groups=groups, tiled=True)
    second, table = pl.pallas_call(
        sum_kernel,
        out_shape=(
            jax.ShapeDtypeStruct((16, 8, D), low),
            jax.ShapeDtypeStruct((HEADS // 2 * QSLOTS, LANES), wide),
        ),
        in_specs=[vmem],
        out_specs=(vmem, vmem),
        compiler_params=pltpu.CompilerParams(vmem_limit_bytes=8 * 2**20),
        cost_estimate=pl.CostEstimate(flops=10**6, bytes_accessed=10**6, transcendentals=0),
    )(got)

    full = jnp.concatenate((lon_out, out_own), axis=2)
    full, second = lax.optimization_barrier((full, second))
    final = lax.all_to_all(second, "lat", 0, 0, tiled=True)
    lat_out = passed_along(full[:, 3:], "lat", 1)
    table, _ = lax.optimization_barrier((table, lat_out))
    table_grad = pl.pallas_call(
        spread_kernel,
        out_shape=jax.ShapeDtypeStruct((HEADS, 1, NBIAS), wide),
        in_specs=[smem, vmem, vmem],
        out_specs=vmem,
        cost_estimate=pl.CostEstimate(flops=10**5, bytes_accessed=10**5, transcendentals=0),
    )(place, table, swapped(table, 1)).transpose(1, 0, 2)
    done = jnp.concatenate((lat_out, full[:, :3]), axis=1).transpose(0, 3, 1, 2, 4)
    output, input_grad = done[0], done[1]
    final, output, input_grad, table_grad = lax.optimization_barrier(
        (final, output, input_grad, table_grad)
    )
    final = jnp.sum(final.astype(wide), axis=0)
    weight_grads, vector_grads = final[:6], final[6:]
    return (output, input_grad, weight_grads, table_grad, vector_grads)


def solution(mesh):
    placed = (
        P(None, "lat", "lon", None),
        P(None, "lat", "lon", None),
        P(None, "lat", "lon"),
        P(),
        P(),
        P(),
        P(),
        P("lat", None, None),
        P(),
    )
    return jax.shard_map(
        local,
        mesh=mesh,
        in_specs=placed,
        out_specs=(
            P(None, "lat", "lon", None),
            P(None, "lat", "lon", None),
            P(("lat", "lon"), None),
            P("lat", None, None),
            P(),
        ),
        check_vma=False,
    )
```

```python
import functools

import jax
import jax.numpy as jnp
from jax import lax
from jax.experimental import pallas as pl
from jax.experimental.pallas import tpu as pltpu
from jax.sharding import PartitionSpec as P

HEADS = 12
HEAD_DIM = 32
WIN_TOK = 144
NBIAS = 759
D = 384
TOK = 288
EPS = 1e-05
BLOCKED = -10000.0
MARK = 256.0
LANES = 128
LOG2E = 1.4426950408889634
QSLOTS = 8
CHUNK = 104

wide = jnp.float32
low = jnp.bfloat16

NN = (((1,), (0,)), ((), ()))
NT = (((1,), (1,)), ((), ()))
TN = (((0,), (0,)), ((), ()))


def mm(a, b, dims):
    return lax.dot_general(a, b, dims, preferred_element_type=wide)


def passed_along(value, axis, steps):
    count = lax.axis_size(axis)
    pairs = [(source, (source + steps) % count) for source in range(count)]
    return lax.ppermute(value, axis, pairs)


def pre_kernel(
    place_ref, table_in, ids_in, bias_ref, order_ref, table_ref, ids_ref, tail_ref, far_ref, sems
):
    copies = [
        pltpu.make_async_copy(table_in, table_ref, sems.at[0]),
        pltpu.make_async_copy(ids_in, ids_ref, sems.at[1]),
    ]
    for copy in copies:
        copy.start()
    new = lax.broadcasted_iota(jnp.int32, (D, D), 0)
    old = lax.broadcasted_iota(jnp.int32, (D, D), 1)
    tens = new // 6
    r = new - 6 * tens
    a = tens & 3
    j = (tens >> 2) & 7
    other = tens >> 5
    core = place_ref[0]
    c = core + other - 2 * core * other
    order_ref[...] = (old == (a * 16 + 2 * j + c) * 6 + r).astype(wide).astype(low)

    for copy in copies:
        copy.wait()
    tail_ref[...] = jnp.zeros((WIN_TOK, LANES), jnp.int32)
    tail_ref[:, 0:16] = ids_ref[:, LANES:WIN_TOK]
    for head in range(HEADS):
        for p in range(6):
            stop = min((p + 1) * LANES, NBIAS)
            far_ref[head * 6 + p : head * 6 + p + 1, 0 : stop - p * LANES] = (
                table_ref[head, :, p * LANES : stop] * LOG2E
            )

    def rows(step, _):
        at = pl.ds(pl.multiple_of(step * 8, 8), 8)
        for half in range(2):
            ids = ids_ref[at, 0:LANES] if half == 0 else tail_ref[at, :]
            place = ids & (LANES - 1)
            piece = ids >> 7
            picks = [piece == p for p in range(6)]
            for head in range(HEADS):
                got = None
                for p in range(6):
                    source = jnp.broadcast_to(
                        far_ref[head * 6 + p : head * 6 + p + 1, :], (8, LANES)
                    )
                    found = jnp.take_along_axis(source, place, axis=1)
                    got = found if got is None else jnp.where(picks[p], found, got)
                bias_ref[head, at, half * LANES : (half + 1) * LANES] = got
        return 0

    lax.fori_loop(0, WIN_TOK // 8, rows, 0)


def main_kernel(
    place_ref,
    scal_ref,
    fields_ref,
    cot_ref,
    lat_ref,
    lon_ref,
    token_ref,
    gain_ref,
    wqkv_in_ref,
    wout_ref,
    bias_ref,
    order_ref,
    filled_ref,
    mixed_ref,
    igrad_ref,
    keep_ref,
    give_ref,
    bgk_ref,
    bgg_ref,
    x_ref,
    c_ref,
    std_ref,
    qkv_ref,
    gm_ref,
    qt_ref,
    gmt_ref,
    gq_ref,
    gkt_ref,
    gvt_ref,
    bg_ref,
    bt_ref,
    wqkv_ref,
    sem,
    mix_ref,
):
    wqkv_copy = pltpu.make_async_copy(wqkv_in_ref, wqkv_ref, sem)
    wqkv_copy.start()
    level = lax.broadcasted_iota(jnp.int32, (4, 1), 0)
    own_masked = jnp.where(level < 2, scal_ref[0], scal_ref[1]) == 1
    for which, own, dest in ((0, fields_ref, x_ref), (1, cot_ref, c_ref)):
        for a in range(6):
            for o in range(12):
                if o >= 6:
                    piece = lon_ref[which, a, o - 6]
                elif a >= 3:
                    piece = lat_ref[which, a - 3, 6 + o]
                else:
                    piece = own[3 + a, 6 + o]
                piece = piece.astype(wide)
                if which == 0 and o < 6 and a < 3:
                    piece = jnp.where(own_masked, MARK, piece)
                base = (a * 12 + o) * 4
                for c in range(3):
                    mix_ref[c, base : base + 4, :] = piece[:, c * LANES : (c + 1) * LANES]
        for zs in range(4):
            for c in range(3):
                dest[zs * 72 : (zs + 1) * 72, c * LANES : (c + 1) * LANES] = mix_ref[
                    c, pl.ds((zs + 1) % 4, 72, stride=4), :
                ]
    raw = x_ref[...]
    masked = raw > 0.5 * MARK
    filled = jnp.where(masked, token_ref[...], raw)
    filled_ref[...] = filled.astype(low)
    gain = gain_ref[...]
    center = filled - jnp.mean(filled, axis=-1, keepdims=True)
    inv_std = lax.rsqrt(jnp.mean(center * center, axis=-1, keepdims=True) + EPS)
    standard = center * inv_std
    std_ref[...] = standard
    normed = (standard * gain).astype(low)
    cot = c_ref[...].astype(low)

    wqkv_copy.wait()
    qkv_ref[...] = mm(normed, wqkv_ref[...], NT).astype(low)
    gm_ref[...] = mm(cot, wout_ref[...], NN).astype(low)
    for w in range(2):
        rows = slice(w * WIN_TOK, (w + 1) * WIN_TOK)
        qt_ref[w] = mm(wqkv_ref[0:D, :], normed[rows], NT).astype(low)
        gmt_ref[w] = mm(wout_ref[...], cot[rows], (((0,), (1,)), ((), ()))).astype(low)

    last = place_ref[1] == 1
    ti = lax.broadcasted_iota(jnp.int32, (WIN_TOK, WIN_TOK), 0)
    tj = lax.broadcasted_iota(jnp.int32, (WIN_TOK, WIN_TOK), 1)
    zi = (ti >= 72).astype(jnp.int32)
    zj = (tj >= 72).astype(jnp.int32)
    ai = (ti - 72 * zi >= 36).astype(jnp.int32)
    aj = (tj - 72 * zj >= 36).astype(jnp.int32)
    lat_apart = jnp.where(last, (ai != aj).astype(wide), 0.0)
    lev_apart = (zi != zj).astype(wide)
    apart = [
        jnp.concatenate([value] * 4, axis=0) > 0.0 for value in (lat_apart, lat_apart + lev_apart)
    ]
    lane = lax.broadcasted_iota(jnp.int32, (1, LANES), 1) // HEAD_DIM
    scale = HEAD_DIM ** (-0.5)
    masks = [(lane == sub).astype(low) for sub in range(4)]
    totals = [None] * HEADS

    def first_products(group, w):
        rows = slice(w * WIN_TOK, (w + 1) * WIN_TOK)
        q = qkv_ref[rows, group * LANES : (group + 1) * LANES]
        k = qkv_ref[rows, D + group * LANES : D + (group + 1) * LANES]
        v = qkv_ref[rows, 2 * D + group * LANES : 2 * D + (group + 1) * LANES]
        g = gm_ref[rows, group * LANES : (group + 1) * LANES]
        g_four = jnp.concatenate([g * mask for mask in masks], axis=0)
        scores = mm(jnp.concatenate([q * mask for mask in masks], axis=0), k, NT)
        return k, v, g_four, scores, mm(g_four, v, NT)

    def weights_of(group, w, k, v, g_four, scores, grad_attn):
        biases = jnp.concatenate(
            [bias_ref[group * 4 + sub, :, 0:WIN_TOK] for sub in range(4)], axis=0
        )
        scores = scores * (scale * LOG2E) + biases
        scores = jnp.where(apart[w], BLOCKED * LOG2E, scores)
        top = jnp.max(scores, axis=-1, keepdims=True)
        expo = jnp.exp2(scores - top)
        prob = (expo * (1.0 / jnp.sum(expo, axis=-1, keepdims=True))).astype(low)
        return k, g_four, grad_attn, prob, mm(prob, v, NN)

    def score_grads(group, w, k, g_four, grad_attn, prob, mixed):
        delta = jnp.sum(g_four.astype(wide) * mixed, axis=-1, keepdims=True)
        grad = prob.astype(wide) * (grad_attn - delta)
        for sub in range(4):
            head = group * 4 + sub
            part = slice(sub * WIN_TOK, (sub + 1) * WIN_TOK)
            if w == 0:
                totals[head] = grad[part]
            else:
                total = totals[head] + grad[part]
                bg_ref[head] = total[:, 0:LANES]
                bt_ref[head, :, 0:16] = total[:, LANES:WIN_TOK]
        return k, prob, mixed, grad.astype(low)

    def last_products(group, w, k, prob, mixed, glow):
        cols = slice(group * LANES, (group + 1) * LANES)
        rows = slice(w * WIN_TOK, (w + 1) * WIN_TOK)
        gq = mm(glow, k, NN)
        mixed_sum = jnp.zeros((WIN_TOK, LANES), wide)
        gq_sum = jnp.zeros((WIN_TOK, LANES), wide)
        for sub in range(4):
            head = group * 4 + sub
            feats = slice(head * HEAD_DIM, (head + 1) * HEAD_DIM)
            part = slice(sub * WIN_TOK, (sub + 1) * WIN_TOK)
            mixed_sum = jnp.where(lane == sub, mixed[part], mixed_sum)
            gq_sum = jnp.where(lane == sub, gq[part], gq_sum)
            gvt_ref[w, feats, :] = mm(gmt_ref[w, feats, :], prob[part], NN).astype(low)
            gkt_ref[w, feats, :] = (mm(qt_ref[w, feats, :], glow[part], NN) * scale).astype(low)
        mixed_ref[rows, cols] = mixed_sum.astype(low)
        gq_ref[rows, cols] = (gq_sum * scale).astype(low)

    work = [(group, w) for group in range(3) for w in range(2)]
    states = [None] * 6
    for n in range(-3, 9):
        if 0 <= n + 1 < 6:
            states[n + 1] = first_products(*work[n + 1])
        if 0 <= n < 6:
            states[n] = weights_of(*work[n], *states[n])
        if 0 <= n - 1 < 6:
            last_products(*work[n - 1], *states[n - 1])
        if 0 <= n < 6:
            states[n] = score_grads(*work[n], *states[n])

    mixed = mixed_ref[...]

    core = place_ref[0]
    for i in range(6):
        halves = []
        for head in (i, i + 6):
            tail = [bt_ref[head, pl.ds(k, 18, stride=8), :][:, 0:16] for k in range(8)]
            blank = jnp.zeros((14, LANES), wide)
            halves.append(
                jnp.concatenate([bg_ref[head], jnp.concatenate(tail, axis=1), blank], axis=0)
            )
        bgk_ref[i] = jnp.where(core == 0, halves[0], halves[1])
        bgg_ref[i] = jnp.where(core == 0, halves[1], halves[0]).astype(low)

    gq = gq_ref[...]
    gk = jnp.concatenate([gkt_ref[w].T for w in range(2)], axis=0)
    gv = jnp.concatenate([gvt_ref[w].T for w in range(2)], axis=0)
    grad_normed = (
        mm(gq, wqkv_ref[0:D, :], NN)
        + mm(gk, wqkv_ref[D : 2 * D, :], NN)
        + mm(gv, wqkv_ref[2 * D : 3 * D, :], NN)
    )
    grad_normed = grad_normed.astype(low).astype(wide)
    standard = std_ref[...]
    scaled = grad_normed * gain
    inner = (
        scaled
        - jnp.mean(scaled, axis=-1, keepdims=True)
        - standard * jnp.mean(scaled * standard, axis=-1, keepdims=True)
    )
    grad_filled = c_ref[...] + inv_std * inner
    igrad_ref[...] = jnp.where(masked, 0.0, grad_filled).astype(low)
    gain_grad = jnp.sum(grad_normed * standard, axis=0, keepdims=True)
    token_grad = jnp.sum(jnp.where(masked, grad_filled, 0.0), axis=0, keepdims=True)

    order = order_ref[...]
    turned = [mm(order, value, NT).astype(low) for value in (gq, gk, gv, cot)]
    parts = [mm(value, normed, NN) for value in turned[:3]] + [mm(turned[3], mixed, NN)]
    vectors = jnp.concatenate([gain_grad, token_grad, jnp.zeros((6, D), wide)], axis=0)
    for n in range(16):
        rows = slice(n * 24, (n + 1) * 24)
        chunk = jnp.concatenate([part[rows] for part in parts] + [vectors], axis=0)
        dest = keep_ref if n < 8 else give_ref
        dest[n % 8] = chunk.astype(low)


def out_kernel(filled_ref, mixed_ref, igrad_ref, wout_ref, out_own_ref, out_lon_ref, mix_ref):
    def put_back(which, value):
        for zs in range(4):
            for c in range(3):
                mix_ref[c, pl.ds((zs + 1) % 4, 72, stride=4), :] = value[
                    zs * 72 : (zs + 1) * 72, c * LANES : (c + 1) * LANES
                ]
        for a in range(6):
            for o in range(12):
                base = (a * 12 + o) * 4
                piece = jnp.concatenate([mix_ref[c, base : base + 4, :] for c in range(3)], axis=1)
                if o < 6:
                    out_own_ref[which, a, o] = piece.astype(low)
                else:
                    out_lon_ref[which, a, o - 6] = piece.astype(low)

    branch = mm(mixed_ref[...], wout_ref[...], NT).astype(low).astype(wide)
    put_back(0, filled_ref[...].astype(wide) + branch)
    put_back(1, igrad_ref[...].astype(wide))


def table_kernel(mine_ref, other_ref, ids_ref, sums_ref, total_ref, near_ref, tail_ref, rest_ref):
    slot = lax.broadcasted_iota(jnp.int32, (2 * QSLOTS, LANES), 0)
    slot = jnp.where(slot < QSLOTS, 2 * slot, 2 * (slot - QSLOTS) + 1)
    spot = lax.broadcasted_iota(jnp.int32, (LANES // 2, LANES), 0)
    near_ref[...] = ids_ref[:, 0:LANES]
    tail_ref[:, 0:16] = ids_ref[:, LANES:WIN_TOK]
    rest_ref[...] = jnp.concatenate(
        [tail_ref[pl.ds(k, 18, stride=8), :][:, 0:16] for k in range(8)], axis=1
    )
    total_ref[...] = mine_ref[...] + other_ref[...].astype(wide)

    def one_step(step, acc):
        lefts = []
        rights = []
        for s in range(9):
            if s < 8:
                row = step * 8 + s
                ids = near_ref[pl.ds(row, 1), :]
            else:
                row = WIN_TOK + step
                ids = rest_ref[pl.ds(step, 1), :]
            vals = [total_ref[head, pl.ds(row, 1), :] for head in range(HEADS // 2)]
            rights.append(((ids & (LANES // 2 - 1)) == spot).astype(wide).astype(low))
            here = (ids >> 6) == slot
            lefts.append(
                jnp.concatenate([jnp.where(here, val, 0.0) for val in vals], axis=0).astype(low)
            )
        left = jnp.concatenate(lefts, axis=1)
        right = jnp.concatenate(rights, axis=1)
        return acc + mm(left, right, NT)

    start = jnp.zeros((HEADS * QSLOTS, LANES // 2), wide)
    acc = lax.fori_loop(0, 18, one_step, start, unroll=18)
    for head in range(HEADS // 2):
        even = acc[2 * QSLOTS * head : 2 * QSLOTS * head + QSLOTS]
        odd = acc[2 * QSLOTS * head + QSLOTS : 2 * QSLOTS * (head + 1)]
        sums_ref[QSLOTS * head : QSLOTS * (head + 1), :] = jnp.concatenate([even, odd], axis=1)


def pack_kernel(keep_ref, taken_ref, table_ref, send_ref):
    total = keep_ref[0].astype(wide) + taken_ref[0].astype(wide)
    table = table_ref[...]
    row = lax.broadcasted_iota(jnp.int32, (HEADS // 2 * QSLOTS, 1), 0)
    for n in range(2):
        for p in range(3):
            piece = total[96 + n : 97 + n, p * LANES : (p + 1) * LANES]
            table = jnp.where(row == QSLOTS * p + 6 + n, piece, table)
    extra = jnp.concatenate([table[0:16], table[16:32], table[32:48]], axis=1).astype(low)
    for m in range(8):
        total = keep_ref[m].astype(wide) + taken_ref[m].astype(wide)
        send_ref[m, 0:96, :] = total[0:96].astype(low)
        send_ref[m, 96:112, :] = extra


def sum_kernel(got_ref, second_ref, table_ref):
    total = got_ref[0].astype(wide)
    for m in range(1, 8):
        total = total + got_ref[m].astype(wide)
    extra = total[96:112]
    table = jnp.concatenate([extra[:, p * LANES : (p + 1) * LANES] for p in range(3)], axis=0)
    table_ref[...] = table
    vectors = jnp.concatenate(
        [table[QSLOTS * p + 6 : QSLOTS * p + 8] for p in range(3)], axis=1
    )
    for a in range(16):
        chunk = jnp.concatenate([total[6 * a : 6 * a + 6], vectors], axis=0)
        second_ref[a] = chunk.astype(low)


def spread_kernel(place_ref, mine_ref, other_ref, table_ref):
    mine = mine_ref[...]
    other = other_ref[...]
    halves = (
        jnp.where(place_ref[0] == 0, mine, other),
        jnp.where(place_ref[0] == 0, other, mine),
    )
    for head in range(HEADS):
        for q in range(6):
            spot = head % 6 * QSLOTS + q
            width = min(LANES, NBIAS - q * LANES)
            piece = halves[head // 6][spot : spot + 1, :]
            table_ref[head, :, q * LANES : q * LANES + width] = piece[:, 0:width]


def local(
    fields,
    cotangent,
    window_mask,
    mask_token,
    norm_gain,
    qkv_weight,
    out_weight,
    bias_table,
    bias_index,
):
    own_mask = window_mask[:, 0, 0]
    last = (lax.axis_index("lat") == lax.axis_size("lat") - 1).astype(jnp.int32)
    core = lax.axis_index("lon") % 2
    place = jnp.stack([core, last])
    fields = fields.transpose(1, 2, 0, 3)
    cotangent = cotangent.transpose(1, 2, 0, 3)
    smem = pl.BlockSpec(memory_space=pltpu.SMEM)
    vmem = pl.BlockSpec(memory_space=pltpu.VMEM)
    hbm = pl.BlockSpec(memory_space=pltpu.HBM)
    hidden = jnp.repeat(own_mask, 2)[:, None] == 1
    strip = jnp.stack((jnp.where(hidden, jnp.bfloat16(MARK), fields[:3]), cotangent[:3]))
    lat_in = passed_along(strip, "lat", -1)
    bias, order = pl.pallas_call(
        pre_kernel,
        out_shape=(
            jax.ShapeDtypeStruct((HEADS, WIN_TOK, 256), wide),
            jax.ShapeDtypeStruct((D, D), low),
        ),
        in_specs=[smem, hbm, hbm],
        out_specs=(vmem,) * 2,
        scratch_shapes=[
            pltpu.VMEM((HEADS, 1, NBIAS), wide),
            pltpu.VMEM((WIN_TOK, WIN_TOK), jnp.int32),
            pltpu.VMEM((WIN_TOK, LANES), jnp.int32),
            pltpu.VMEM((HEADS * 6, LANES), wide),
            pltpu.SemaphoreType.DMA((2,)),
        ],
        compiler_params=pltpu.CompilerParams(vmem_limit_bytes=8 * 2**20),
        cost_estimate=pl.CostEstimate(flops=5 * 10**9, bytes_accessed=0, transcendentals=0),
    )(place, bias_table.transpose(1, 0, 2), bias_index)
    lat_in, bias, order = lax.optimization_barrier((lat_in, bias, order))
    own = jnp.stack((jnp.where(hidden, jnp.bfloat16(MARK), fields[3:, :6]), cotangent[3:, :6]))
    lon_in = passed_along(jnp.concatenate((own, lat_in[:, :, :6]), axis=1), "lon", -1)

    filled, mixed, igrad, keep, give, pairs, pairs_give = pl.pallas_call(
        main_kernel,
        out_shape=(
            jax.ShapeDtypeStruct((TOK, D), low),
            jax.ShapeDtypeStruct((TOK, D), low),
            jax.ShapeDtypeStruct((TOK, D), low),
            jax.ShapeDtypeStruct((8, CHUNK, D), low),
            jax.ShapeDtypeStruct((8, CHUNK, D), low),
            jax.ShapeDtypeStruct((HEADS // 2, 176, LANES), wide),
            jax.ShapeDtypeStruct((HEADS // 2, 176, LANES), low),
        ),
        in_specs=[smem, smem] + [vmem] * 6 + [hbm, vmem, vmem, vmem],
        out_specs=(vmem,) * 7,
        scratch_shapes=[
            pltpu.VMEM((TOK, D), wide),
            pltpu.VMEM((TOK, D), wide),
            pltpu.VMEM((TOK, D), wide),
            pltpu.VMEM((TOK, 3 * D), low),
            pltpu.VMEM((TOK, D), low),
            pltpu.VMEM((2, D, WIN_TOK), low),
            pltpu.VMEM((2, D, WIN_TOK), low),
            pltpu.VMEM((TOK, D), low),
            pltpu.VMEM((2, D, WIN_TOK), low),
            pltpu.VMEM((2, D, WIN_TOK), low),
            pltpu.VMEM((HEADS, WIN_TOK, LANES), wide),
            pltpu.VMEM((HEADS, WIN_TOK, LANES), wide),
            pltpu.VMEM((3 * D, D), low),
            pltpu.SemaphoreType.DMA(()),
            pltpu.VMEM((3, TOK, LANES), wide),
        ],
        compiler_params=pltpu.CompilerParams(vmem_limit_bytes=24 * 2**20),
        cost_estimate=pl.CostEstimate(
            flops=10**10, bytes_accessed=0, transcendentals=0
        ),
    )(
        place,
        own_mask,
        fields,
        cotangent,
        lat_in,
        lon_in,
        mask_token.astype(wide)[None],
        norm_gain.astype(wide)[None],
        qkv_weight,
        out_weight,
        bias,
        order,
    )

    size = lax.axis_size("lon")

    def swapped(value, bit):
        return lax.ppermute(value, "lon", [(i, i ^ bit) for i in range(size)])

    out_own, out_lon = pl.pallas_call(
        out_kernel,
        out_shape=(
            jax.ShapeDtypeStruct((2, 6, 6, 4, D), low),
            jax.ShapeDtypeStruct((2, 6, 6, 4, D), low),
        ),
        in_specs=[vmem] * 4,
        out_specs=(vmem, vmem),
        scratch_shapes=[pltpu.VMEM((3, TOK, LANES), wide)],
        compiler_params=pltpu.CompilerParams(vmem_limit_bytes=16 * 2**20),
        cost_estimate=pl.CostEstimate(flops=2 * 10**9, bytes_accessed=0, transcendentals=0),
    )(filled, mixed, igrad, out_weight)
    lon_out = passed_along(out_lon, "lon", 1)
    other_pairs = swapped(pairs_give, 1)
    taken = swapped(give, 1)
    pairs, out_own = lax.optimization_barrier((pairs, out_own))
    table = pl.pallas_call(
        table_kernel,
        out_shape=jax.ShapeDtypeStruct((HEADS // 2 * QSLOTS, LANES), wide),
        in_specs=[vmem] * 3,
        out_specs=vmem,
        scratch_shapes=[
            pltpu.VMEM((HEADS // 2, 176, LANES), wide),
            pltpu.VMEM((WIN_TOK, LANES), jnp.int32),
            pltpu.VMEM((WIN_TOK, LANES), jnp.int32),
            pltpu.VMEM((18, LANES), jnp.int32),
        ],
        compiler_params=pltpu.CompilerParams(vmem_limit_bytes=8 * 2**20),
        cost_estimate=pl.CostEstimate(flops=10**9, bytes_accessed=10**6, transcendentals=0),
    )(pairs, other_pairs, bias_index)
    pair = pl.pallas_call(
        pack_kernel,
        out_shape=jax.ShapeDtypeStruct((8, 112, D), low),
        in_specs=[vmem] * 3,
        out_specs=vmem,
        compiler_params=pltpu.CompilerParams(vmem_limit_bytes=8 * 2**20),
        cost_estimate=pl.CostEstimate(flops=10**6, bytes_accessed=10**6, transcendentals=0),
    )(keep, taken, table)
    pair, lon_out = lax.optimization_barrier((pair, lon_out))
    groups = [list(range(c, size, 2)) for c in range(2)]
    got = lax.all_to_all(pair, "lon", 0, 0, axis_index_groups=groups, tiled=True)
    second, table = pl.pallas_call(
        sum_kernel,
        out_shape=(
            jax.ShapeDtypeStruct((16, 8, D), low),
            jax.ShapeDtypeStruct((HEADS // 2 * QSLOTS, LANES), wide),
        ),
        in_specs=[vmem],
        out_specs=(vmem, vmem),
        compiler_params=pltpu.CompilerParams(vmem_limit_bytes=8 * 2**20),
        cost_estimate=pl.CostEstimate(flops=10**6, bytes_accessed=10**6, transcendentals=0),
    )(got)

    full = jnp.concatenate((lon_out, out_own), axis=2)
    full, second = lax.optimization_barrier((full, second))
    final = lax.all_to_all(second, "lat", 0, 0, tiled=True)
    lat_out = passed_along(full[:, 3:], "lat", 1)
    table, _ = lax.optimization_barrier((table, lat_out))
    table_grad = pl.pallas_call(
        spread_kernel,
        out_shape=jax.ShapeDtypeStruct((HEADS, 1, NBIAS), wide),
        in_specs=[smem, vmem, vmem],
        out_specs=vmem,
        cost_estimate=pl.CostEstimate(flops=10**5, bytes_accessed=10**5, transcendentals=0),
    )(place, table, swapped(table, 1)).transpose(1, 0, 2)
    done = jnp.concatenate((lat_out, full[:, :3]), axis=1).transpose(0, 3, 1, 2, 4)
    output, input_grad = done[0], done[1]
    final, output, input_grad, table_grad = lax.optimization_barrier(
        (final, output, input_grad, table_grad)
    )
    final = jnp.sum(final.astype(wide), axis=0)
    weight_grads, vector_grads = final[:6], final[6:]
    return (output, input_grad, weight_grads, table_grad, vector_grads)


def solution(mesh):
    placed = (
        P(None, "lat", "lon", None),
        P(None, "lat", "lon", None),
        P(None, "lat", "lon"),
        P(),
        P(),
        P(),
        P(),
        P("lat", None, None),
        P(),
    )
    return jax.shard_map(
        local,
        mesh=mesh,
        in_specs=placed,
        out_specs=(
            P(None, "lat", "lon", None),
            P(None, "lat", "lon", None),
            P(("lat", "lon"), None),
            P("lat", None, None),
            P(),
        ),
        check_vma=False,
    )
```
